512 devices in a mesh: orient: 8 (over z_lo, x), tile: 64 (over y, z_hi, core).
Axes of the slice: x: 4, y: 8, z: 8 (z_hi: 4, z_lo: 2; z = z_hi * 2 + z_lo), core: 2. Of those that a mesh axis runs over, the one named last changes fastest.
Arguments:
- image_tiles: bfloat16 [64, 512, 512], P('tile'), may hold values from -6 to 6
- templates: bfloat16 [8, 64, 384, 384], P('orient', 'tile'), may hold values from -0.015625 to 0.015625
- owners: int32 [8, 2], P('orient'), may hold values from 0 to 63, as said below
Outputs:
- corr_sum: float32 [64, 512, 512], P('tile', 'orient')
- corr_sumsq: float32 [64, 512, 512], P('tile', 'orient')
- corr_max: float32 [64, 512, 512], P('tile', 'orient')
The draws below stay inside these ranges and needn't reach their ends.
Inputs may be any that keep to these rules, and one draw needn't show every extreme that they name: Within a group the 2 owners are distinct.
All inputs are finite; a program needn't handle non-finite values.
Results may differ from the reference program's by a relative error of at most 0.02.
Values may be sent and summed in bfloat16 or wider, within the bound.
No kernel may reach another device: no remote copies, remote signals or barrier semaphores. Data moves between devices by JAX's collectives and lax.ppermute only.
A program may use at most 64 MiB of HBM per device.

```python
import jax
import jax.numpy as jnp
from jax import lax

NP = 512
M = 384
STEPS = 2
GROUPS = 8
HOLDERS = 64


def draw_owners(key, part):
    key = jax.random.fold_in(key, 7)
    key_rows, key_first, key_flip = jax.random.split(key, 3)
    keys_all = jax.random.split(key_rows, GROUPS)
    picked = jax.vmap(lambda one: jax.random.permutation(one, HOLDERS)[:STEPS])(keys_all)
    picked = picked.astype(jnp.int32)
    middle = (jax.random.permutation(key_first, HOLDERS - 2) + 1).astype(jnp.int32)
    flipped = jax.random.randint(key_flip, (), 0, 2).astype(jnp.int32)
    first_end = flipped * (HOLDERS - 1)
    second_end = HOLDERS - 1 - first_end
    ends = jnp.stack([first_end, second_end]).astype(jnp.int32)
    first_row = jnp.concatenate([ends, middle])[:STEPS]
    return picked.at[0].set(first_row).astype(jnp.int32)


def block_levels(rng, extent, shards, smallest, top_value):
    def one(dim, blocks):
        heights = jax.random.uniform(jax.random.fold_in(jax.random.fold_in(rng, 6), dim), (blocks,), jnp.float32, smallest / len(shards), top_value / len(shards))
        return jnp.repeat(jnp.exp(heights), extent[dim] // blocks).reshape((-1,) + (1,) * (len(extent) - dim - 1))

    level = one(*shards[0])
    for cut in shards[1:]:
        level = level * one(*cut)
    return level


def bell_draw(own_key, extent, scale, reach, cuts=(), kind=jnp.bfloat16):
    factor_of = block_levels(own_key, extent, cuts, -0.22, 0.18) if cuts else 1.0
    values = jax.random.normal(own_key, extent, jnp.float32) * scale * factor_of
    return jnp.minimum(jnp.maximum(values, -reach), reach).astype(kind)


def setup_inputs(seed: int = 0) -> dict:
    seeds = jax.random.split(jax.random.key(seed), 4)
    image_tiles = bell_draw(seeds[0], (HOLDERS, NP, NP), 1.0, 6.0, ((0, 64),))
    templates = bell_draw(seeds[1], (GROUPS, HOLDERS, M, M), (M * M) ** -0.5, 0.015625, ((0, 8), (1, 64)))
    owners = draw_owners(jax.random.fold_in(seeds[3], 71), 0)
    return dict(image_tiles=image_tiles, templates=templates, owners=owners)


def make_tables(size):
    index_line = jnp.arange(size, dtype=jnp.int32)
    phases = (index_line[:, None] * index_line[None, :]) % size
    angles = phases.astype(jnp.float32) * (2.0 * 3.141592653589793 / size)
    return jnp.cos(angles).astype(jnp.bfloat16), jnp.sin(angles).astype(jnp.bfloat16)


def matmul(left, right):
    return jnp.dot(left, right, preferred_element_type=jnp.float32)


def forward_image(field, cos_table, sin_table):
    first_a = matmul(cos_table, field).astype(jnp.bfloat16)
    first_b = matmul(sin_table, field).astype(jnp.bfloat16)
    spec_re = (matmul(first_a, cos_table) - matmul(first_b, sin_table)).astype(jnp.bfloat16)
    spec_im = (-(matmul(first_a, sin_table) + matmul(first_b, cos_table))).astype(jnp.bfloat16)
    return spec_re, spec_im


def forward_template(template, cos_table, sin_table):
    width = template.shape[0]
    cos_left = cos_table[:, :width]
    sin_left = sin_table[:, :width]
    first_a = matmul(cos_left, template).astype(jnp.bfloat16)
    first_b = matmul(sin_left, template).astype(jnp.bfloat16)
    cos_top = cos_table[:width, :]
    sin_top = sin_table[:width, :]
    spec_re = (matmul(first_a, cos_top) - matmul(first_b, sin_top)).astype(jnp.bfloat16)
    spec_im = (-(matmul(first_a, sin_top) + matmul(first_b, cos_top))).astype(jnp.bfloat16)
    return spec_re, spec_im


def correlate(image_re, image_im, tmpl_re, tmpl_im, cos_table, sin_table):
    size = image_re.shape[0]
    ire = image_re.astype(jnp.float32)
    iim = image_im.astype(jnp.float32)
    tre = tmpl_re.astype(jnp.float32)
    tim = tmpl_im.astype(jnp.float32)
    prod_re = (ire * tre + iim * tim).astype(jnp.bfloat16)
    prod_im = (iim * tre - ire * tim).astype(jnp.bfloat16)
    back_re = (matmul(cos_table, prod_re) - matmul(sin_table, prod_im)).astype(jnp.bfloat16)
    back_im = (matmul(cos_table, prod_im) + matmul(sin_table, prod_re)).astype(jnp.bfloat16)
    scale = jnp.float32(1.0 / (size * size))
    return (matmul(back_re, cos_table) - matmul(back_im, sin_table)) * scale


def reference(image_tiles, templates, owners):
    cos_table, sin_table = make_tables(NP)
    group_index = jnp.arange(GROUPS, dtype=jnp.int32)
    chosen = templates[group_index[:, None], owners]
    chosen = chosen.reshape(GROUPS * STEPS, M, M)
    tmpl_re, tmpl_im = lax.map(lambda one: forward_template(one, cos_table, sin_table), chosen)

    def per_tile(field):
        image_re, image_im = forward_image(field, cos_table, sin_table)

        def accumulate(carry, spectra):
            total, squares, largest = carry
            values = correlate(image_re, image_im, spectra[0], spectra[1], cos_table, sin_table)
            return (total + values, squares + values * values, jnp.maximum(largest, values)), None

        start = (jnp.zeros((NP, NP), jnp.float32), jnp.zeros((NP, NP), jnp.float32),
                 jnp.full((NP, NP), -jnp.inf, jnp.float32))
        result, unused = lax.scan(accumulate, start, (tmpl_re, tmpl_im))
        return result

    corr_sum, corr_sumsq, corr_max = lax.map(per_tile, image_tiles)
    return corr_sum, corr_sumsq, corr_max
```

```python
import numpy as np
import jax
import jax.numpy as jnp
from jax import lax
from jax.experimental import pallas as pl
from jax.experimental.pallas import tpu as pltpu
from jax.sharding import PartitionSpec as P

STEPS = 2
NP = 512
HALF = NP // 2
M = 384
REST = M - HALF
Y, Z, CORES = 8, 4, 2
PLANE = Y * CORES
CHUNK = M // PLANE


def make_tables():
    line = np.arange(NP)
    phases = (line[:, None] * line[None, :]) % NP
    angles = phases.astype(np.float32) * np.float32(2.0 * 3.141592653589793 / NP)
    cos_table, sin_table = np.cos(angles), np.sin(angles)
    tables = []
    for parity in (0, 1):
        cos_part = cos_table[parity::2, :HALF]
        sin_part = sin_table[parity::2, :HALF]
        tables.append(np.block([[cos_part, sin_part], [-sin_part, cos_part]]))
    tables = np.stack(tables).astype(jnp.bfloat16)
    return tables, np.ascontiguousarray(tables.transpose(0, 2, 1))


def matmul(left, right):
    return jnp.dot(left, right, preferred_element_type=jnp.float32)


def right_transform(stacked, table):
    return matmul(stacked[:HALF], table[:HALF]) + matmul(stacked[HALF:], table[HALF:])


def wide(values):
    return values.astype(jnp.float32)


def narrow(values):
    return values.astype(jnp.bfloat16)


def combine(left, right, parity):
    return left + right if parity == 0 else left - right


def image_kernel(field_ref, fwd_ref, inv_ref, spec_ref):
    top_left, top_right = wide(field_ref[:HALF, :HALF]), wide(field_ref[:HALF, HALF:])
    low_left, low_right = wide(field_ref[HALF:, :HALF]), wide(field_ref[HALF:, HALF:])
    for row_parity in (0, 1):
        left = combine(top_left, low_left, row_parity)
        right = combine(top_right, low_right, row_parity)
        for col_parity in (0, 1):
            folded = narrow(combine(left, right, col_parity))
            first = narrow(matmul(fwd_ref[row_parity, :, :HALF], folded))
            spec_ref[row_parity, col_parity] = narrow(right_transform(first, inv_ref[col_parity]))


def correlate_kernel(parts_ref, spec_ref, fwd_ref, inv_ref, out_ref, field_ref, back_ref):
    for step in range(STEPS):
        for part in range(PLANE):
            rows = slice(part * CHUNK, (part + 1) * CHUNK)
            values = wide(parts_ref[part, step])
            field_ref[step, rows, :] = values if step == 0 else -values
    for row_parity in (0, 1):
        rows_folded = []
        for step in range(STEPS):
            top = combine(field_ref[step, :REST], field_ref[step, HALF:], row_parity)
            rows_folded.append((top, field_ref[step, REST:HALF]))
        for col_parity in (0, 1):
            pieces = []
            for step in range(STEPS):
                for block in rows_folded[step]:
                    left = combine(block[:, :REST], block[:, HALF:], col_parity)
                    pieces.append(narrow(jnp.concatenate([left, block[:, REST:HALF]], axis=1)))
            first = narrow(matmul(fwd_ref[row_parity], jnp.concatenate(pieces, axis=0)))
            tmpl = right_transform(first, inv_ref[col_parity])
            tmpl_re, tmpl_im = tmpl[:, :HALF], tmpl[:, HALF:]
            image_re = wide(spec_ref[row_parity, col_parity, :, :HALF])
            image_im = wide(spec_ref[row_parity, col_parity, :, HALF:])
            prod_re = narrow(image_re * tmpl_re + image_im * tmpl_im)
            prod_im = narrow(image_im * tmpl_re - image_re * tmpl_im)
            back = narrow(matmul(inv_ref[row_parity], jnp.concatenate([prod_re, prod_im], axis=0)))
            back_ref[row_parity, col_parity] = right_transform(back, fwd_ref[col_parity])
    blocks, _, rows_out, _ = out_ref.shape
    for step in range(STEPS):
        cols = slice(step * HALF, (step + 1) * HALF)
        for block in range(blocks // 2):
            rows = slice(block * rows_out, (block + 1) * rows_out)
            even_even, even_odd = back_ref[0, 0, rows, cols], back_ref[0, 1, rows, cols]
            odd_even, odd_odd = back_ref[1, 0, rows, cols], back_ref[1, 1, rows, cols]
            even_left, odd_left = even_even + even_odd, odd_even + odd_odd
            even_right, odd_right = even_even - even_odd, odd_even - odd_odd
            out_ref[block, step, :, :HALF] = narrow(even_left + odd_left)
            out_ref[block, step, :, HALF:] = narrow(even_right + odd_right)
            out_ref[block + blocks // 2, step, :, :HALF] = narrow(even_left - odd_left)
            out_ref[block + blocks // 2, step, :, HALF:] = narrow(even_right - odd_right)


def statistics_kernel(values_ref, total_ref, squares_ref, largest_ref):
    scale = jnp.float32(1.0 / (NP * NP))
    total = squares = largest = None
    for group in range(values_ref.shape[0]):
        for step in range(STEPS):
            values = wide(values_ref[group, step]) * scale
            if total is None:
                total, squares, largest = values, values * values, values
            else:
                total = total + values
                squares = squares + values * values
                largest = jnp.maximum(largest, values)
    total_ref[0] = total
    squares_ref[0] = squares
    largest_ref[0] = largest


def call(kernel, name, outs, scratch, *operands):
    whole = pl.BlockSpec(memory_space=pltpu.VMEM)
    return pl.pallas_call(
        kernel,
        name=name,
        out_shape=outs,
        in_specs=[whole] * len(operands),
        out_specs=jax.tree.map(lambda _: whole, outs),
        scratch_shapes=scratch,
        compiler_params=pltpu.CompilerParams(vmem_limit_bytes=32 * 1024 * 1024),
    )(*operands)


def share_templates(own_template, owners):
    tile_index = lax.axis_index("tile")
    planes = [[(y * Z + z) * CORES + c for y in range(Y) for c in range(CORES)] for z in range(Z)]
    columns = [[(y * Z + z) * CORES + c for z in range(Z)] for y in range(Y) for c in range(CORES)]
    owner_z = owners // CORES % Z
    owner_place = owners // (Z * CORES) * CORES + owners % CORES
    shares = lax.all_to_all(
        own_template.reshape(PLANE, CHUNK, M), "tile", 0, 0, axis_index_groups=planes
    )
    kept = jnp.stack([shares[owner_place[step]] for step in range(STEPS)])
    spread = jnp.broadcast_to(kept[None], (Z, *kept.shape))
    spread = lax.all_to_all(spread, "tile", 0, 0, axis_index_groups=columns)
    kept = jnp.stack([spread[owner_z[step], step] for step in range(STEPS)])
    spread = jnp.broadcast_to(kept[None], (PLANE, *kept.shape))
    return lax.all_to_all(spread, "tile", 0, 0, axis_index_groups=planes)


def per_device(image_tiles, templates, owners):
    fwd, inv = (jnp.asarray(table) for table in make_tables())
    groups_here = lax.axis_size("orient")
    rows_out = NP // groups_here
    quarter = (2, 2, HALF, NP)
    spec = call(
        image_kernel, "image_spectrum", jax.ShapeDtypeStruct(quarter, jnp.bfloat16), [], image_tiles[0], fwd, inv
    )
    parts = share_templates(templates[0, 0], owners[0])
    values = call(
        correlate_kernel,
        "correlate",
        jax.ShapeDtypeStruct((groups_here, STEPS, rows_out, NP), jnp.bfloat16),
        [pltpu.VMEM((STEPS, M, M), jnp.float32), pltpu.VMEM(quarter, jnp.float32)],
        parts,
        spec,
        fwd,
        inv,
    )
    values = lax.all_to_all(values, "orient", 0, 0)
    out = jax.ShapeDtypeStruct((1, rows_out, NP), jnp.float32)
    return call(statistics_kernel, "statistics", (out, out, out), [], values)


def solution(mesh):
    placed = (P("tile", None, None), P("orient", "tile", None, None), P("orient", None))
    return jax.shard_map(
        per_device,
        mesh=mesh,
        in_specs=placed,
        out_specs=(P("tile", "orient", None), P("tile", "orient", None), P("tile", "orient", None)),
        check_vma=False,
    )
```

```python
import numpy as np
import jax
import jax.numpy as jnp
from jax import lax
from jax.experimental import pallas as pl
from jax.experimental.pallas import tpu as pltpu
from jax.sharding import PartitionSpec as P

STEPS = 2
NP = 512
HALF = NP // 2
M = 384
REST = M - HALF
Y, Z, CORES = 8, 4, 2
PLANE = Y * CORES
CHUNK = M // PLANE


def make_tables():
    line = np.arange(NP)
    phases = (line[:, None] * line[None, :]) % NP
    angles = phases.astype(np.float32) * np.float32(2.0 * 3.141592653589793 / NP)
    cos_table, sin_table = np.cos(angles), np.sin(angles)
    tables = []
    for parity in (0, 1):
        cos_part = cos_table[parity::2, :HALF]
        sin_part = sin_table[parity::2, :HALF]
        tables.append(np.block([[cos_part, sin_part], [-sin_part, cos_part]]))
    tables = np.stack(tables).astype(jnp.bfloat16)
    return tables, np.ascontiguousarray(tables.transpose(0, 2, 1))


def matmul(left, right):
    return jnp.dot(left, right, preferred_element_type=jnp.float32)


def wide(values):
    return values.astype(jnp.float32)


def narrow(values):
    return values.astype(jnp.bfloat16)


def combine(left, right, parity):
    return left + right if parity == 0 else left - right


def pick(shares_ref, place_ref, step):
    total = None
    for place in range(shares_ref.shape[0]):
        share = shares_ref[place, step] if len(shares_ref.shape) == 4 else shares_ref[place]
        here = jnp.where(place_ref[step : step + 1] == place, 1.0, 0.0)
        total = wide(share) * here if total is None else total + wide(share) * here
    return narrow(total)


def pick_place_kernel(shares_ref, place_ref, out_ref):
    for step in range(STEPS):
        share = pick(shares_ref, place_ref, step)
        for receiver in range(out_ref.shape[0]):
            out_ref[receiver, step] = share


def pick_plane_kernel(shares_ref, place_ref, out_ref):
    for step in range(STEPS):
        share = pick(shares_ref, place_ref, step)
        for receiver in range(step, out_ref.shape[0], CORES):
            out_ref[receiver] = share


def side_by_side(left, col_parity):
    cols = slice(col_parity * HALF, (col_parity + 1) * HALF)
    return jnp.concatenate([jnp.concatenate([a[:HALF, cols], a[HALF:, cols]], axis=1) for a in left], axis=0)


def image_kernel(first_ref, second_ref, fwd_ref, inv_ref, spec_ref):
    quarters = []
    for field in (first_ref, second_ref):
        top_left, top_right = wide(field[:HALF, :HALF]), wide(field[:HALF, HALF:])
        low_left, low_right = wide(field[HALF:, :HALF]), wide(field[HALF:, HALF:])
        quarters.append((top_left, top_right, low_left, low_right))
    left = []
    for row_parity in (0, 1):
        folded = []
        for col_parity in (0, 1):
            parts = []
            for top_left, top_right, low_left, low_right in quarters:
                left_half = combine(top_left, low_left, row_parity)
                right_half = combine(top_right, low_right, row_parity)
                parts.append(narrow(combine(left_half, right_half, col_parity)))
            folded.append(jnp.concatenate(parts, axis=0))
        left.append(narrow(matmul(fwd_ref[row_parity], jnp.concatenate(folded, axis=1))))
    for col_parity in (0, 1):
        spec_ref[col_parity] = narrow(matmul(side_by_side(left, col_parity), inv_ref[col_parity]))


def correlate_kernel(shares_ref, spec_ref, fwd_ref, inv_ref, out_ref, field_ref, back_ref):
    for place in range(PLANE):
        field_ref[place * CHUNK : (place + 1) * CHUNK, :] = wide(shares_ref[place])
    left = []
    for row_parity in (0, 1):
        top = combine(field_ref[:REST], field_ref[HALF:], row_parity)
        rows = jnp.concatenate([top, field_ref[REST:HALF]], axis=0)
        folded = []
        for col_parity in (0, 1):
            first = combine(rows[:, :REST], rows[:, HALF:], col_parity)
            folded.append(narrow(jnp.concatenate([first, rows[:, REST:HALF]], axis=1)))
        left.append(narrow(matmul(fwd_ref[row_parity, :, :HALF], jnp.concatenate(folded, axis=1))))
    products = []
    for col_parity in (0, 1):
        tmpl = matmul(side_by_side(left, col_parity), inv_ref[col_parity])
        tmpl_re, tmpl_im = tmpl[:, :HALF], tmpl[:, HALF:]
        image_re, image_im = wide(spec_ref[col_parity, :, :HALF]), wide(spec_ref[col_parity, :, HALF:])
        prod_re = narrow(image_re * tmpl_re + image_im * tmpl_im)
        prod_im = narrow(image_im * tmpl_re - image_re * tmpl_im)
        products.append((prod_re, prod_im))
    left = []
    for row_parity in (0, 1):
        rows = slice(row_parity * HALF, (row_parity + 1) * HALF)
        stacked = [jnp.concatenate([prod_re[rows], prod_im[rows]], axis=0) for prod_re, prod_im in products]
        left.append(narrow(matmul(inv_ref[row_parity], jnp.concatenate(stacked, axis=1))))
    for col_parity in (0, 1):
        back_ref[col_parity] = matmul(side_by_side(left, col_parity), fwd_ref[col_parity])
    rows_out = out_ref.shape[1]
    groups = NP // rows_out
    for core in range(CORES):
        cols = slice(core * HALF, (core + 1) * HALF)
        for group in range(groups // 2):
            even = slice(group * rows_out, (group + 1) * rows_out)
            odd = slice(HALF + group * rows_out, HALF + (group + 1) * rows_out)
            even_even, even_odd = back_ref[0, even, cols], back_ref[1, even, cols]
            odd_even, odd_odd = back_ref[0, odd, cols], back_ref[1, odd, cols]
            even_left, odd_left = even_even + even_odd, odd_even + odd_odd
            even_right, odd_right = even_even - even_odd, odd_even - odd_odd
            upper = group * CORES + core
            lower = upper + groups // 2 * CORES
            out_ref[upper, :, :HALF] = narrow(even_left + odd_left)
            out_ref[upper, :, HALF:] = narrow(even_right + odd_right)
            out_ref[lower, :, :HALF] = narrow(even_left - odd_left)
            out_ref[lower, :, HALF:] = narrow(even_right - odd_right)


def pairwise(op, values):
    while len(values) > 1:
        values = [op(*values[i : i + 2]) for i in range(0, len(values), 2)]
    return values[0]


def statistics_kernel(values_ref, total_ref, squares_ref, largest_ref):
    scale = 1.0 / (NP * NP)
    count, height, width = values_ref.shape
    for row in range(0, height, 16):
        for col in range(0, width, 128):
            rows, cols = slice(row, row + 16), slice(col, col + 128)
            values = [wide(values_ref[template, rows, cols]) for template in range(count)]
            total_ref[0, rows, cols] = pairwise(jnp.add, values) * jnp.float32(scale)
            squares_ref[0, rows, cols] = pairwise(jnp.add, [v * v for v in values]) * jnp.float32(scale * scale)
            largest_ref[0, rows, cols] = pairwise(jnp.maximum, values) * jnp.float32(scale)


def call(kernel, name, outs, scratch, *operands):
    whole = pl.BlockSpec(memory_space=pltpu.VMEM)
    return pl.pallas_call(
        kernel,
        name=name,
        out_shape=outs,
        in_specs=[whole] * len(operands),
        out_specs=jax.tree.map(lambda _: whole, outs),
        scratch_shapes=scratch,
        compiler_params=pltpu.CompilerParams(vmem_limit_bytes=32 * 1024 * 1024),
    )(*operands)


def receive_template(own_template, owners):
    planes = [[(y * Z + z) * CORES + c for y in range(Y) for c in range(CORES)] for z in range(Z)]
    columns = [[(y * Z + z) * CORES + c for z in range(Z)] for y in range(Y) for c in range(CORES)]
    owner_z = owners // CORES % Z
    owner_place = owners // (Z * CORES) * CORES + owners % CORES
    owner_z, owner_place = (jnp.broadcast_to(place[:, None], (STEPS, M)) for place in (owner_z, owner_place))
    shares = own_template.reshape(PLANE, CHUNK, M)
    shares = lax.all_to_all(shares, "tile", 0, 0, axis_index_groups=planes)
    spread = jax.ShapeDtypeStruct((Z, STEPS, CHUNK, M), jnp.bfloat16)
    shares = call(pick_place_kernel, "pick_place", spread, [], shares, owner_place)
    shares = lax.all_to_all(shares, "tile", 0, 0, axis_index_groups=columns)
    spread = jax.ShapeDtypeStruct((PLANE, CHUNK, M), jnp.bfloat16)
    shares = call(pick_plane_kernel, "pick_plane", spread, [], shares, owner_z)
    return lax.all_to_all(shares, "tile", 0, 0, axis_index_groups=planes)


def image_fields(own_tile):
    tiles = lax.axis_size("tile")
    is_first = lax.axis_index("tile") % CORES == 0
    other_tile = lax.ppermute(own_tile, "tile", [(tile, tile ^ 1) for tile in range(tiles)])
    return jnp.where(is_first, own_tile, other_tile), jnp.where(is_first, other_tile, own_tile)


def per_device(image_tiles, templates, owners):
    fwd, inv = (jnp.asarray(table) for table in make_tables())
    groups_here = lax.axis_size("orient")
    tiles = lax.axis_size("tile")
    rows_out = NP // groups_here
    spectrum = (2, NP, NP)
    fields = image_fields(image_tiles[0])
    spec = call(image_kernel, "image_spectrum", jax.ShapeDtypeStruct(spectrum, jnp.bfloat16), [], *fields, fwd, inv)
    shares = receive_template(templates[0, 0], owners[0])
    values = call(
        correlate_kernel,
        "correlate",
        jax.ShapeDtypeStruct((groups_here * CORES, rows_out, NP), jnp.bfloat16),
        [pltpu.VMEM((M, M), jnp.float32), pltpu.VMEM(spectrum, jnp.float32)],
        shares,
        spec,
        fwd,
        inv,
    )
    across = [
        [group * tiles + pair * CORES + c for group in range(groups_here) for c in range(CORES)]
        for pair in range(tiles // CORES)
    ]
    values = lax.all_to_all(values, ("orient", "tile"), 0, 0, axis_index_groups=across)
    out = jax.ShapeDtypeStruct((1, rows_out, NP), jnp.float32)
    return call(statistics_kernel, "statistics", (out, out, out), [], values)


def solution(mesh):
    placed = (P("tile", None, None), P("orient", "tile", None, None), P("orient", None))
    return jax.shard_map(
        per_device,
        mesh=mesh,
        in_specs=placed,
        out_specs=(P("tile", "orient", None), P("tile", "orient", None), P("tile", "orient", None)),
        check_vma=False,
    )
```

```python
import numpy as np
import jax
import jax.numpy as jnp
from jax import lax
from jax.experimental import pallas as pl
from jax.experimental.pallas import tpu as pltpu
from jax.sharding import PartitionSpec as P

STEPS = 2
NP = 512
HALF = NP // 2
M = 384
REST = M - HALF
Y, Z, CORES = 8, 4, 2
PLANE = Y * CORES
CHUNK = M // PLANE


def make_tables():
    line = np.arange(NP)
    phases = (line[:, None] * line[None, :]) % NP
    angles = phases.astype(np.float32) * np.float32(2.0 * 3.141592653589793 / NP)
    cos_table, sin_table = np.cos(angles), np.sin(angles)
    tables = []
    for parity in (0, 1):
        cos_part = cos_table[parity::2, :HALF]
        sin_part = sin_table[parity::2, :HALF]
        tables.append(np.block([[cos_part, sin_part], [-sin_part, cos_part]]))
    tables = np.stack(tables).astype(jnp.bfloat16)
    return tables, np.ascontiguousarray(tables.transpose(0, 2, 1))


def matmul(left, right):
    return jnp.dot(left, right, preferred_element_type=jnp.float32)


def wide(values):
    return values.astype(jnp.float32)


def narrow(values):
    return values.astype(jnp.bfloat16)


def combine(left, right, parity):
    return left + right if parity == 0 else left - right


def pick(shares_ref, place_ref, step):
    total = None
    for place in range(shares_ref.shape[0]):
        share = shares_ref[place, step] if len(shares_ref.shape) == 4 else shares_ref[place]
        here = jnp.where(place_ref[step : step + 1] == place, 1.0, 0.0)
        total = wide(share) * here if total is None else total + wide(share) * here
    return narrow(total)


def pick_place_kernel(shares_ref, place_ref, out_ref):
    for step in range(STEPS):
        share = pick(shares_ref, place_ref, step)
        for receiver in range(out_ref.shape[0]):
            out_ref[receiver, step] = share


def pick_plane_kernel(shares_ref, place_ref, out_ref):
    for step in range(STEPS):
        share = pick(shares_ref, place_ref, step)
        for y in range(Y):
            out_ref[plane_place(y, step)] = share


def side_by_side(left, col_parity):
    cols = slice(col_parity * HALF, (col_parity + 1) * HALF)
    return jnp.concatenate([jnp.concatenate([a[:HALF, cols], a[HALF:, cols]], axis=1) for a in left], axis=0)


def image_kernel(first_ref, second_ref, fwd_ref, inv_ref, spec_ref):
    quarters = []
    for field in (first_ref, second_ref):
        top_left, top_right = wide(field[:HALF, :HALF]), wide(field[:HALF, HALF:])
        low_left, low_right = wide(field[HALF:, :HALF]), wide(field[HALF:, HALF:])
        quarters.append((top_left, top_right, low_left, low_right))
    left = []
    for row_parity in (0, 1):
        folded = []
        for col_parity in (0, 1):
            parts = []
            for top_left, top_right, low_left, low_right in quarters:
                left_half = combine(top_left, low_left, row_parity)
                right_half = combine(top_right, low_right, row_parity)
                parts.append(narrow(combine(left_half, right_half, col_parity)))
            folded.append(jnp.concatenate(parts, axis=0))
        left.append(narrow(matmul(fwd_ref[row_parity], jnp.concatenate(folded, axis=1))))
    for col_parity in (0, 1):
        spec_ref[col_parity] = narrow(matmul(side_by_side(left, col_parity), inv_ref[col_parity]))


def correlate_kernel(shares_ref, spec_ref, fwd_ref, inv_ref, out_ref, field_ref, back_ref):
    for place in range(PLANE):
        field_ref[place * CHUNK : (place + 1) * CHUNK, :] = wide(shares_ref[place])
    left = []
    for row_parity in (0, 1):
        top = combine(field_ref[:REST], field_ref[HALF:], row_parity)
        rows = jnp.concatenate([top, field_ref[REST:HALF]], axis=0)
        folded = []
        for col_parity in (0, 1):
            first = combine(rows[:, :REST], rows[:, HALF:], col_parity)
            folded.append(narrow(jnp.concatenate([first, rows[:, REST:HALF]], axis=1)))
        left.append(narrow(matmul(fwd_ref[row_parity, :, :HALF], jnp.concatenate(folded, axis=1))))
    products = []
    for col_parity in (0, 1):
        tmpl = matmul(side_by_side(left, col_parity), inv_ref[col_parity])
        tmpl_re, tmpl_im = tmpl[:, :HALF], tmpl[:, HALF:]
        image_re, image_im = wide(spec_ref[col_parity, :, :HALF]), wide(spec_ref[col_parity, :, HALF:])
        prod_re = narrow(image_re * tmpl_re + image_im * tmpl_im)
        prod_im = narrow(image_im * tmpl_re - image_re * tmpl_im)
        products.append((prod_re, prod_im))
    left = []
    for row_parity in (0, 1):
        rows = slice(row_parity * HALF, (row_parity + 1) * HALF)
        stacked = [jnp.concatenate([prod_re[rows], prod_im[rows]], axis=0) for prod_re, prod_im in products]
        left.append(narrow(matmul(inv_ref[row_parity], jnp.concatenate(stacked, axis=1))))
    for col_parity in (0, 1):
        back_ref[col_parity] = matmul(side_by_side(left, col_parity), fwd_ref[col_parity])
    rows_out = out_ref.shape[1]
    groups = NP // rows_out
    members = result_members()
    for core in range(CORES):
        cols = slice(core * HALF, (core + 1) * HALF)
        for group in range(groups // 2):
            even = slice(group * rows_out, (group + 1) * rows_out)
            odd = slice(HALF + group * rows_out, HALF + (group + 1) * rows_out)
            even_even, even_odd = back_ref[0, even, cols], back_ref[1, even, cols]
            odd_even, odd_odd = back_ref[0, odd, cols], back_ref[1, odd, cols]
            even_left, odd_left = even_even + even_odd, odd_even + odd_odd
            even_right, odd_right = even_even - even_odd, odd_even - odd_odd
            upper = members.index((group, core))
            lower = members.index((group + groups // 2, core))
            out_ref[upper, :, :HALF] = narrow(even_left + odd_left)
            out_ref[upper, :, HALF:] = narrow(even_right + odd_right)
            out_ref[lower, :, :HALF] = narrow(even_left - odd_left)
            out_ref[lower, :, HALF:] = narrow(even_right - odd_right)


def pairwise(op, values):
    while len(values) > 1:
        values = [op(*values[i : i + 2]) for i in range(0, len(values), 2)]
    return values[0]


def statistics_kernel(values_ref, total_ref, squares_ref, largest_ref):
    scale = 1.0 / (NP * NP)
    count, height, width = values_ref.shape
    for row in range(0, height, 16):
        for col in range(0, width, 128):
            rows, cols = slice(row, row + 16), slice(col, col + 128)
            values = [wide(values_ref[template, rows, cols]) for template in range(count)]
            total_ref[0, rows, cols] = pairwise(jnp.add, values) * jnp.float32(scale)
            squares_ref[0, rows, cols] = pairwise(jnp.add, [v * v for v in values]) * jnp.float32(scale * scale)
            largest_ref[0, rows, cols] = pairwise(jnp.maximum, values) * jnp.float32(scale)


def call(kernel, name, outs, scratch, *operands):
    whole = pl.BlockSpec(memory_space=pltpu.VMEM)
    return pl.pallas_call(
        kernel,
        name=name,
        out_shape=outs,
        in_specs=[whole] * len(operands),
        out_specs=jax.tree.map(lambda _: whole, outs),
        scratch_shapes=scratch,
        compiler_params=pltpu.CompilerParams(vmem_limit_bytes=32 * 1024 * 1024),
    )(*operands)


def plane_place(y, core):
    return (3 * y + 4) % Y * CORES + core


def column_place(z):
    return (z + 2) % Z


def result_members():
    return [(zl * 4 + (x + 2) % 4, c) for zl in range(2) for x in range(4) for c in range(CORES)]


def receive_template(own_template, owners):
    plane_members = sorted(((y, c) for y in range(Y) for c in range(CORES)), key=lambda member: plane_place(*member))
    planes = [[(y * Z + z) * CORES + c for y, c in plane_members] for z in range(Z)]
    columns = [[(y * Z + z) * CORES + c for z in sorted(range(Z), key=column_place)] for y in range(Y) for c in range(CORES)]
    owner_z = column_place(owners // CORES % Z)
    owner_place = plane_place(owners // (Z * CORES), owners % CORES)
    owner_z, owner_place = (jnp.broadcast_to(place[:, None], (STEPS, M)) for place in (owner_z, owner_place))
    shares = own_template.reshape(PLANE, CHUNK, M)
    shares = lax.all_to_all(shares, "tile", 0, 0, axis_index_groups=planes)
    spread = jax.ShapeDtypeStruct((Z, STEPS, CHUNK, M), jnp.bfloat16)
    shares = call(pick_place_kernel, "pick_place", spread, [], shares, owner_place)
    shares = lax.all_to_all(shares, "tile", 0, 0, axis_index_groups=columns)
    spread = jax.ShapeDtypeStruct((PLANE, CHUNK, M), jnp.bfloat16)
    shares = call(pick_plane_kernel, "pick_plane", spread, [], shares, owner_z)
    return lax.all_to_all(shares, "tile", 0, 0, axis_index_groups=planes)


def image_fields(own_tile):
    tiles = lax.axis_size("tile")
    is_first = lax.axis_index("tile") % CORES == 0
    other_tile = lax.ppermute(own_tile, "tile", [(tile, tile ^ 1) for tile in range(tiles)])
    return jnp.where(is_first, own_tile, other_tile), jnp.where(is_first, other_tile, own_tile)


def per_device(image_tiles, templates, owners):
    fwd, inv = (jnp.asarray(table) for table in make_tables())
    groups_here = lax.axis_size("orient")
    tiles = lax.axis_size("tile")
    rows_out = NP // groups_here
    spectrum = (2, NP, NP)
    fields = image_fields(image_tiles[0])
    spec = call(image_kernel, "image_spectrum", jax.ShapeDtypeStruct(spectrum, jnp.bfloat16), [], *fields, fwd, inv)
    shares = receive_template(templates[0, 0], owners[0])
    values = call(
        correlate_kernel,
        "correlate",
        jax.ShapeDtypeStruct((groups_here * CORES, rows_out, NP), jnp.bfloat16),
        [pltpu.VMEM((M, M), jnp.float32), pltpu.VMEM(spectrum, jnp.float32)],
        shares,
        spec,
        fwd,
        inv,
    )
    across = [[group * tiles + pair * CORES + c for group, c in result_members()] for pair in range(tiles // CORES)]
    values = lax.all_to_all(values, ("orient", "tile"), 0, 0, axis_index_groups=across)
    out = jax.ShapeDtypeStruct((1, rows_out, NP), jnp.float32)
    return call(statistics_kernel, "statistics", (out, out, out), [], values)


def solution(mesh):
    placed = (P("tile", None, None), P("orient", "tile", None, None), P("orient", None))
    return jax.shard_map(
        per_device,
        mesh=mesh,
        in_specs=placed,
        out_specs=(P("tile", "orient", None), P("tile", "orient", None), P("tile", "orient", None)),
        check_vma=False,
    )
```

```python
import numpy as np
import jax
import jax.numpy as jnp
from jax import lax
from jax.experimental import pallas as pl
from jax.experimental.pallas import tpu as pltpu
from jax.sharding import PartitionSpec as P

STEPS = 2
NP = 512
HALF = NP // 2
M = 384
REST = M - HALF
Y, Z, CORES = 8, 4, 2
PLANE = Y * CORES
CHUNK = M // PLANE


def make_tables():
    line = np.arange(NP)
    phases = (line[:, None] * line[None, :]) % NP
    angles = phases.astype(np.float32) * np.float32(2.0 * 3.141592653589793 / NP)
    cos_table, sin_table = np.cos(angles), np.sin(angles)
    tables = []
    for parity in (0, 1):
        cos_part = cos_table[parity::2, :HALF]
        sin_part = sin_table[parity::2, :HALF]
        tables.append(np.block([[cos_part, sin_part], [-sin_part, cos_part]]))
    tables = np.stack(tables).astype(jnp.bfloat16)
    return tables, np.ascontiguousarray(tables.transpose(0, 2, 1))


def matmul(left, right):
    return jnp.dot(left, right, preferred_element_type=jnp.float32)


def wide(values):
    return values.astype(jnp.float32)


def narrow(values):
    return values.astype(jnp.bfloat16)


def combine(left, right, parity):
    return left + right if parity == 0 else left - right


def pick(shares_ref, place_ref, step):
    total = None
    for place in range(shares_ref.shape[0]):
        share = shares_ref[place, step] if len(shares_ref.shape) == 4 else shares_ref[place]
        here = jnp.where(place_ref[step : step + 1] == place, 1.0, 0.0)
        total = wide(share) * here if total is None else total + wide(share) * here
    return narrow(total)


def pick_place_kernel(shares_ref, place_ref, out_ref):
    for step in range(STEPS):
        share = pick(shares_ref, place_ref, step)
        for receiver in range(out_ref.shape[0]):
            out_ref[receiver, step] = share


def pick_plane_kernel(shares_ref, place_ref, out_ref):
    for step in range(STEPS):
        share = pick(shares_ref, place_ref, step)
        for y in range(Y):
            out_ref[gather_members().index((y, step))] = share


def side_by_side(left, col_parity):
    cols = slice(col_parity * HALF, (col_parity + 1) * HALF)
    return jnp.concatenate([jnp.concatenate([a[:HALF, cols], a[HALF:, cols]], axis=1) for a in left], axis=0)


def image_kernel(top_ref, low_ref, fwd_ref, inv_ref, spec_ref):
    quarters = []
    for core in range(CORES):
        top_left, top_right = wide(top_ref[core, :, :HALF]), wide(top_ref[core, :, HALF:])
        low_left, low_right = wide(low_ref[core, :, :HALF]), wide(low_ref[core, :, HALF:])
        quarters.append((top_left, top_right, low_left, low_right))
    left = []
    for row_parity in (0, 1):
        folded = []
        for col_parity in (0, 1):
            parts = []
            for top_left, top_right, low_left, low_right in quarters:
                left_half = combine(top_left, low_left, row_parity)
                right_half = combine(top_right, low_right, row_parity)
                parts.append(narrow(combine(left_half, right_half, col_parity)))
            folded.append(jnp.concatenate(parts, axis=0))
        left.append(narrow(matmul(fwd_ref[row_parity], jnp.concatenate(folded, axis=1))))
    for col_parity in (0, 1):
        spec_ref[col_parity] = narrow(matmul(side_by_side(left, col_parity), inv_ref[col_parity]))


def correlate_kernel(shares_ref, spec_ref, fwd_ref, inv_ref, out_ref, field_ref, back_ref):
    for source, member in enumerate(gather_members()):
        place = plane_place(*member)
        field_ref[place * CHUNK : (place + 1) * CHUNK, :] = wide(shares_ref[source])
    left = []
    for row_parity in (0, 1):
        top = combine(field_ref[:REST], field_ref[HALF:], row_parity)
        rows = jnp.concatenate([top, field_ref[REST:HALF]], axis=0)
        folded = []
        for col_parity in (0, 1):
            first = combine(rows[:, :REST], rows[:, HALF:], col_parity)
            folded.append(narrow(jnp.concatenate([first, rows[:, REST:HALF]], axis=1)))
        left.append(narrow(matmul(fwd_ref[row_parity, :, :HALF], jnp.concatenate(folded, axis=1))))
    products = []
    for col_parity in (0, 1):
        tmpl = matmul(side_by_side(left, col_parity), inv_ref[col_parity])
        tmpl_re, tmpl_im = tmpl[:, :HALF], tmpl[:, HALF:]
        image_re, image_im = wide(spec_ref[col_parity, :, :HALF]), wide(spec_ref[col_parity, :, HALF:])
        prod_re = narrow(image_re * tmpl_re + image_im * tmpl_im)
        prod_im = narrow(image_im * tmpl_re - image_re * tmpl_im)
        products.append((prod_re, prod_im))
    left = []
    for row_parity in (0, 1):
        rows = slice(row_parity * HALF, (row_parity + 1) * HALF)
        stacked = [jnp.concatenate([prod_re[rows], prod_im[rows]], axis=0) for prod_re, prod_im in products]
        left.append(narrow(matmul(inv_ref[row_parity], jnp.concatenate(stacked, axis=1))))
    for col_parity in (0, 1):
        back_ref[col_parity] = matmul(side_by_side(left, col_parity), fwd_ref[col_parity])
    rows_out = out_ref.shape[1]
    groups = NP // rows_out
    members = result_members()
    for core in range(CORES):
        cols = slice(core * HALF, (core + 1) * HALF)
        for group in range(groups // 2):
            even = slice(group * rows_out, (group + 1) * rows_out)
            odd = slice(HALF + group * rows_out, HALF + (group + 1) * rows_out)
            even_even, even_odd = back_ref[0, even, cols], back_ref[1, even, cols]
            odd_even, odd_odd = back_ref[0, odd, cols], back_ref[1, odd, cols]
            even_left, odd_left = even_even + even_odd, odd_even + odd_odd
            even_right, odd_right = even_even - even_odd, odd_even - odd_odd
            upper = members.index((group, core))
            lower = members.index((group + groups // 2, core))
            out_ref[upper, :, :HALF] = narrow(even_left + odd_left)
            out_ref[upper, :, HALF:] = narrow(even_right + odd_right)
            out_ref[lower, :, :HALF] = narrow(even_left - odd_left)
            out_ref[lower, :, HALF:] = narrow(even_right - odd_right)


def pairwise(op, values):
    while len(values) > 1:
        values = [op(*values[i : i + 2]) for i in range(0, len(values), 2)]
    return values[0]


def statistics_kernel(values_ref, total_ref, squares_ref, largest_ref):
    scale = 1.0 / (NP * NP)
    count, height, width = values_ref.shape
    for row in range(0, height, 16):
        for col in range(0, width, 128):
            rows, cols = slice(row, row + 16), slice(col, col + 128)
            values = [wide(values_ref[template, rows, cols]) for template in range(count)]
            total_ref[0, rows, cols] = pairwise(jnp.add, values) * jnp.float32(scale)
            squares_ref[0, rows, cols] = pairwise(jnp.add, [v * v for v in values]) * jnp.float32(scale * scale)
            largest_ref[0, rows, cols] = pairwise(jnp.maximum, values) * jnp.float32(scale)


def call(kernel, name, outs, scratch, *operands):
    whole = pl.BlockSpec(memory_space=pltpu.VMEM)
    return pl.pallas_call(
        kernel,
        name=name,
        out_shape=outs,
        in_specs=[whole] * len(operands),
        out_specs=jax.tree.map(lambda _: whole, outs),
        scratch_shapes=scratch,
        compiler_params=pltpu.CompilerParams(vmem_limit_bytes=32 * 1024 * 1024),
    )(*operands)


def plane_place(y, core):
    return (3 * y + 4) % Y * CORES + core


def gather_members():
    return sorted(((y, c) for y in range(Y) for c in range(CORES)), key=lambda member: plane_place(*member))


def column_place(z):
    return (z + 2) % Z


def result_members():
    return [(zl * 4 + (x + 2) % 4, c) for x in range(4) for c in range(CORES) for zl in range(2)]


def receive_template(own_template, owners, spec):
    plane_members = sorted(((y, c) for y in range(Y) for c in range(CORES)), key=lambda member: plane_place(*member))
    planes = [[(y * Z + z) * CORES + c for y, c in plane_members] for z in range(Z)]
    gather_planes = [[(y * Z + z) * CORES + c for y, c in gather_members()] for z in range(Z)]
    columns = [[(y * Z + z) * CORES + c for z in sorted(range(Z), key=column_place)] for y in range(Y) for c in range(CORES)]
    owner_z = column_place(owners // CORES % Z)
    owner_place = plane_place(owners // (Z * CORES), owners % CORES)
    owner_z, owner_place = (jnp.broadcast_to(place[:, None], (STEPS, M)) for place in (owner_z, owner_place))
    shares = own_template.reshape(PLANE, CHUNK, M)
    shares = lax.all_to_all(shares, "tile", 0, 0, axis_index_groups=planes)
    shares, spec = lax.optimization_barrier((shares, spec))
    spread = jax.ShapeDtypeStruct((Z, STEPS, CHUNK, M), jnp.bfloat16)
    shares = call(pick_place_kernel, "pick_place", spread, [], shares, owner_place)
    shares = lax.all_to_all(shares, "tile", 0, 0, axis_index_groups=columns)
    spread = jax.ShapeDtypeStruct((PLANE, CHUNK, M), jnp.bfloat16)
    shares = call(pick_plane_kernel, "pick_plane", spread, [], shares, owner_z)
    return lax.all_to_all(shares, "tile", 0, 0, axis_index_groups=gather_planes), spec


def image_fields(own_tile):
    pairs = [[tile, tile + 1] for tile in range(0, lax.axis_size("tile"), CORES)]
    halves = [lax.all_gather(half, "tile", axis_index_groups=pairs) for half in (own_tile[:HALF], own_tile[HALF:])]
    return halves


def per_device(image_tiles, templates, owners):
    fwd, inv = (jnp.asarray(table) for table in make_tables())
    groups_here = lax.axis_size("orient")
    tiles = lax.axis_size("tile")
    rows_out = NP // groups_here
    spectrum = (2, NP, NP)
    fields = image_fields(image_tiles[0])
    spec = call(image_kernel, "image_spectrum", jax.ShapeDtypeStruct(spectrum, jnp.bfloat16), [], *fields, fwd, inv)
    shares, spec = receive_template(templates[0, 0], owners[0], spec)
    values = call(
        correlate_kernel,
        "correlate",
        jax.ShapeDtypeStruct((groups_here * CORES, rows_out, NP), jnp.bfloat16),
        [pltpu.VMEM((M, M), jnp.float32), pltpu.VMEM(spectrum, jnp.float32)],
        shares,
        spec,
        fwd,
        inv,
    )
    across = [[group * tiles + pair * CORES + c for group, c in result_members()] for pair in range(tiles // CORES)]
    values = lax.all_to_all(values, ("orient", "tile"), 0, 0, axis_index_groups=across)
    out = jax.ShapeDtypeStruct((1, rows_out, NP), jnp.float32)
    return call(statistics_kernel, "statistics", (out, out, out), [], values)


def solution(mesh):
    placed = (P("tile", None, None), P("orient", "tile", None, None), P("orient", None))
    return jax.shard_map(
        per_device,
        mesh=mesh,
        in_specs=placed,
        out_specs=(P("tile", "orient", None), P("tile", "orient", None), P("tile", "orient", None)),
        check_vma=False,
    )
```

```python
import numpy as np
import jax
import jax.numpy as jnp
from jax import lax
from jax.experimental import pallas as pl
from jax.experimental.pallas import tpu as pltpu
from jax.sharding import PartitionSpec as P

STEPS = 2
NP = 512
HALF = NP // 2
M = 384
REST = M - HALF
Y, Z, CORES = 8, 4, 2
PLANE = Y * CORES
CHUNK = M // PLANE


def make_tables():
    line = np.arange(NP)
    phases = (line[:, None] * line[None, :]) % NP
    angles = phases.astype(np.float32) * np.float32(2.0 * 3.141592653589793 / NP)
    cos_table, sin_table = np.cos(angles), np.sin(angles)
    tables = []
    for parity in (0, 1):
        cos_part = cos_table[parity::2, :HALF]
        sin_part = sin_table[parity::2, :HALF]
        tables.append(np.block([[cos_part, sin_part], [-sin_part, cos_part]]))
    tables = np.stack(tables).astype(jnp.bfloat16)
    return tables, np.ascontiguousarray(tables.transpose(0, 2, 1))


def matmul(left, right):
    return jnp.dot(left, right, preferred_element_type=jnp.float32)


def wide(values):
    return values.astype(jnp.float32)


def narrow(values):
    return values.astype(jnp.bfloat16)


def combine(left, right, parity):
    return left + right if parity == 0 else left - right


def pick(shares_ref, place_ref, step):
    total = None
    for place in range(shares_ref.shape[0]):
        share = shares_ref[place, step] if len(shares_ref.shape) == 4 else shares_ref[place]
        here = jnp.where(place_ref[step : step + 1] == place, 1.0, 0.0)
        total = wide(share) * here if total is None else total + wide(share) * here
    return narrow(total)


def pick_place_kernel(shares_ref, place_ref, out_ref):
    for step in range(STEPS):
        share = pick(shares_ref, place_ref, step)
        for receiver in range(out_ref.shape[0]):
            out_ref[receiver, step] = share


def pick_plane_kernel(shares_ref, place_ref, out_ref):
    for step in range(STEPS):
        share = pick(shares_ref, place_ref, step)
        for y in range(Y):
            out_ref[gather_members().index((y, step))] = share


def side_by_side(left, col_parity):
    cols = slice(col_parity * HALF, (col_parity + 1) * HALF)
    return jnp.concatenate([jnp.concatenate([a[:HALF, cols], a[HALF:, cols]], axis=1) for a in left], axis=0)


def image_kernel(top_ref, low_ref, fwd_ref, inv_ref, spec_ref):
    quarters = []
    for core in range(CORES):
        top_left, top_right = wide(top_ref[core, :, :HALF]), wide(top_ref[core, :, HALF:])
        low_left, low_right = wide(low_ref[core, :, :HALF]), wide(low_ref[core, :, HALF:])
        quarters.append((top_left, top_right, low_left, low_right))
    left = []
    for row_parity in (0, 1):
        folded = []
        for col_parity in (0, 1):
            parts = []
            for top_left, top_right, low_left, low_right in quarters:
                left_half = combine(top_left, low_left, row_parity)
                right_half = combine(top_right, low_right, row_parity)
                parts.append(narrow(combine(left_half, right_half, col_parity)))
            folded.append(jnp.concatenate(parts, axis=0))
        left.append(narrow(matmul(fwd_ref[row_parity], jnp.concatenate(folded, axis=1))))
    for col_parity in (0, 1):
        spec_ref[col_parity] = narrow(matmul(side_by_side(left, col_parity), inv_ref[col_parity]))


def correlate_kernel(shares_ref, spec_ref, fwd_ref, inv_ref, out_ref, field_ref, back_ref):
    for source, member in enumerate(gather_members()):
        place = plane_place(*member)
        field_ref[place * CHUNK : (place + 1) * CHUNK, :] = wide(shares_ref[source])
    left = []
    for row_parity in (0, 1):
        top = combine(field_ref[:REST], field_ref[HALF:], row_parity)
        rows = jnp.concatenate([top, field_ref[REST:HALF]], axis=0)
        folded = []
        for col_parity in (0, 1):
            first = combine(rows[:, :REST], rows[:, HALF:], col_parity)
            folded.append(narrow(jnp.concatenate([first, rows[:, REST:HALF]], axis=1)))
        left.append(narrow(matmul(fwd_ref[row_parity, :, :HALF], jnp.concatenate(folded, axis=1))))
    products = []
    for col_parity in (0, 1):
        tmpl = matmul(side_by_side(left, col_parity), inv_ref[col_parity])
        tmpl_re, tmpl_im = tmpl[:, :HALF], tmpl[:, HALF:]
        image_re, image_im = wide(spec_ref[col_parity, :, :HALF]), wide(spec_ref[col_parity, :, HALF:])
        prod_re = narrow(image_re * tmpl_re + image_im * tmpl_im)
        prod_im = narrow(image_im * tmpl_re - image_re * tmpl_im)
        products.append((prod_re, prod_im))
    left = []
    for row_parity in (0, 1):
        rows = slice(row_parity * HALF, (row_parity + 1) * HALF)
        stacked = [jnp.concatenate([prod_re[rows], prod_im[rows]], axis=0) for prod_re, prod_im in products]
        left.append(narrow(matmul(inv_ref[row_parity], jnp.concatenate(stacked, axis=1))))
    for col_parity in (0, 1):
        back_ref[col_parity] = matmul(side_by_side(left, col_parity), fwd_ref[col_parity])
    rows_out = out_ref.shape[1]
    groups = NP // rows_out
    members = result_members()
    for core in range(CORES):
        cols = slice(core * HALF, (core + 1) * HALF)
        for group in range(groups // 2):
            even = slice(group * rows_out, (group + 1) * rows_out)
            odd = slice(HALF + group * rows_out, HALF + (group + 1) * rows_out)
            even_even, even_odd = back_ref[0, even, cols], back_ref[1, even, cols]
            odd_even, odd_odd = back_ref[0, odd, cols], back_ref[1, odd, cols]
            even_left, odd_left = even_even + even_odd, odd_even + odd_odd
            even_right, odd_right = even_even - even_odd, odd_even - odd_odd
            upper = members.index((group, core))
            lower = members.index((group + groups // 2, core))
            out_ref[upper, :, :HALF] = narrow(even_left + odd_left)
            out_ref[upper, :, HALF:] = narrow(even_right + odd_right)
            out_ref[lower, :, :HALF] = narrow(even_left - odd_left)
            out_ref[lower, :, HALF:] = narrow(even_right - odd_right)


def pairwise(op, values):
    while len(values) > 1:
        values = [op(*values[i : i + 2]) for i in range(0, len(values), 2)]
    return values[0]


def statistics_kernel(values_ref, total_ref, squares_ref, largest_ref):
    scale = 1.0 / (NP * NP)
    count, height, width = values_ref.shape
    for row in range(0, height, 16):
        for col in range(0, width, 128):
            rows, cols = slice(row, row + 16), slice(col, col + 128)
            values = [wide(values_ref[template, rows, cols]) for template in range(count)]
            total_ref[0, rows, cols] = pairwise(jnp.add, values) * jnp.float32(scale)
            squares_ref[0, rows, cols] = pairwise(jnp.add, [v * v for v in values]) * jnp.float32(scale * scale)
            largest_ref[0, rows, cols] = pairwise(jnp.maximum, values) * jnp.float32(scale)


def call(kernel, name, outs, scratch, *operands):
    whole = pl.BlockSpec(memory_space=pltpu.VMEM)
    return pl.pallas_call(
        kernel,
        name=name,
        out_shape=outs,
        in_specs=[whole] * len(operands),
        out_specs=jax.tree.map(lambda _: whole, outs),
        scratch_shapes=scratch,
        compiler_params=pltpu.CompilerParams(vmem_limit_bytes=32 * 1024 * 1024),
    )(*operands)


def plane_place(y, core):
    return (3 * y + 4) % Y * CORES + core


def gather_members():
    return sorted(((y, c) for y in range(Y) for c in range(CORES)), key=lambda member: plane_place(*member))


def column_place(z):
    return (z + 2) % Z


def result_members():
    return [(zl * 4 + x, c) for x in (2, 3, 0, 1) for c in (1, 0) for zl in (1, 0)]


def receive_template(own_template, owners, spec):
    plane_members = sorted(((y, c) for y in range(Y) for c in range(CORES)), key=lambda member: plane_place(*member))
    planes = [[(y * Z + z) * CORES + c for y, c in plane_members] for z in range(Z)]
    gather_planes = [[(y * Z + z) * CORES + c for y, c in gather_members()] for z in range(Z)]
    columns = [[(y * Z + z) * CORES + c for z in sorted(range(Z), key=column_place)] for y in range(Y) for c in range(CORES)]
    owner_z = column_place(owners // CORES % Z)
    owner_place = plane_place(owners // (Z * CORES), owners % CORES)
    owner_z, owner_place = (jnp.broadcast_to(place[:, None], (STEPS, M)) for place in (owner_z, owner_place))
    shares = own_template.reshape(PLANE, CHUNK, M)
    shares = lax.all_to_all(shares, "tile", 0, 0, axis_index_groups=planes)
    shares, spec = lax.optimization_barrier((shares, spec))
    spread = jax.ShapeDtypeStruct((Z, STEPS, CHUNK, M), jnp.bfloat16)
    shares = call(pick_place_kernel, "pick_place", spread, [], shares, owner_place)
    shares = lax.all_to_all(shares, "tile", 0, 0, axis_index_groups=columns)
    spread = jax.ShapeDtypeStruct((PLANE, CHUNK, M), jnp.bfloat16)
    shares = call(pick_plane_kernel, "pick_plane", spread, [], shares, owner_z)
    return lax.all_to_all(shares, "tile", 0, 0, axis_index_groups=gather_planes), spec


def image_fields(own_tile):
    pairs = [[tile, tile + 1] for tile in range(0, lax.axis_size("tile"), CORES)]
    halves = [lax.all_gather(half, "tile", axis_index_groups=pairs) for half in (own_tile[:HALF], own_tile[HALF:])]
    return halves


def per_device(image_tiles, templates, owners):
    fwd, inv = (jnp.asarray(table) for table in make_tables())
    groups_here = lax.axis_size("orient")
    tiles = lax.axis_size("tile")
    rows_out = NP // groups_here
    spectrum = (2, NP, NP)
    fields = image_fields(image_tiles[0])
    spec = call(image_kernel, "image_spectrum", jax.ShapeDtypeStruct(spectrum, jnp.bfloat16), [], *fields, fwd, inv)
    shares, spec = receive_template(templates[0, 0], owners[0], spec)
    values = call(
        correlate_kernel,
        "correlate",
        jax.ShapeDtypeStruct((groups_here * CORES, rows_out, NP), jnp.bfloat16),
        [pltpu.VMEM((M, M), jnp.float32), pltpu.VMEM(spectrum, jnp.float32)],
        shares,
        spec,
        fwd,
        inv,
    )
    across = [[group * tiles + pair * CORES + c for group, c in result_members()] for pair in range(tiles // CORES)]
    values = lax.all_to_all(values, ("orient", "tile"), 0, 0, axis_index_groups=across)
    out = jax.ShapeDtypeStruct((1, rows_out, NP), jnp.float32)
    return call(statistics_kernel, "statistics", (out, out, out), [], values)


def solution(mesh):
    placed = (P("tile", None, None), P("orient", "tile", None, None), P("orient", None))
    return jax.shard_map(
        per_device,
        mesh=mesh,
        in_specs=placed,
        out_specs=(P("tile", "orient", None), P("tile", "orient", None), P("tile", "orient", None)),
        check_vma=False,
    )
```

```python
import numpy as np
import jax
import jax.numpy as jnp
from jax import lax
from jax.experimental import pallas as pl
from jax.experimental.pallas import tpu as pltpu
from jax.sharding import PartitionSpec as P

STEPS = 2
NP = 512
HALF = NP // 2
M = 384
REST = M - HALF
Y, Z, CORES = 8, 4, 2
PLANE = Y * CORES
CHUNK = M // PLANE


def make_tables():
    line = np.arange(NP)
    phases = (line[:, None] * line[None, :]) % NP
    angles = phases.astype(np.float32) * np.float32(2.0 * 3.141592653589793 / NP)
    cos_table, sin_table = np.cos(angles), np.sin(angles)
    tables = []
    for parity in (0, 1):
        cos_part = cos_table[parity::2, :HALF]
        sin_part = sin_table[parity::2, :HALF]
        tables.append(np.block([[cos_part, sin_part], [-sin_part, cos_part]]))
    tables = np.stack(tables).astype(jnp.bfloat16)
    return tables, np.ascontiguousarray(tables.transpose(0, 2, 1))


def matmul(left, right):
    return jnp.dot(left, right, preferred_element_type=jnp.float32)


def wide(values):
    return values.astype(jnp.float32)


def narrow(values):
    return values.astype(jnp.bfloat16)


def combine(left, right, parity):
    return left + right if parity == 0 else left - right


def pick(shares_ref, place_ref, step):
    total = None
    for place in range(shares_ref.shape[0]):
        share = shares_ref[place, step] if len(shares_ref.shape) == 4 else shares_ref[place]
        here = jnp.where(place_ref[step : step + 1] == place, 1.0, 0.0)
        total = wide(share) * here if total is None else total + wide(share) * here
    return narrow(total)


def pick_place_kernel(shares_ref, place_ref, out_ref):
    for step in range(STEPS):
        share = pick(shares_ref, place_ref, step)
        for receiver in range(out_ref.shape[0]):
            out_ref[receiver, step] = share


def pick_plane_kernel(shares_ref, place_ref, out_ref):
    for step in range(STEPS):
        share = pick(shares_ref, place_ref, step)
        for y in range(Y):
            out_ref[plane_place(y, step)] = share


def side_by_side(left, col_parity):
    cols = slice(col_parity * HALF, (col_parity + 1) * HALF)
    return jnp.concatenate([jnp.concatenate([a[:HALF, cols], a[HALF:, cols]], axis=1) for a in left], axis=0)


def image_kernel(top_ref, low_ref, fwd_ref, inv_ref, spec_ref):
    quarters = []
    for core in range(CORES):
        top_left, top_right = wide(top_ref[core, :, :HALF]), wide(top_ref[core, :, HALF:])
        low_left, low_right = wide(low_ref[core, :, :HALF]), wide(low_ref[core, :, HALF:])
        quarters.append((top_left, top_right, low_left, low_right))
    left = []
    for row_parity in (0, 1):
        folded = []
        for col_parity in (0, 1):
            parts = []
            for top_left, top_right, low_left, low_right in quarters:
                left_half = combine(top_left, low_left, row_parity)
                right_half = combine(top_right, low_right, row_parity)
                parts.append(narrow(combine(left_half, right_half, col_parity)))
            folded.append(jnp.concatenate(parts, axis=0))
        left.append(narrow(matmul(fwd_ref[row_parity], jnp.concatenate(folded, axis=1))))
    for col_parity in (0, 1):
        spec_ref[col_parity] = narrow(matmul(side_by_side(left, col_parity), inv_ref[col_parity]))


def correlate_kernel(shares_ref, spec_ref, fwd_ref, inv_ref, out_ref, field_ref, back_ref):
    for place in range(PLANE):
        field_ref[place * CHUNK : (place + 1) * CHUNK, :] = wide(shares_ref[place])
    left = []
    for row_parity in (0, 1):
        top = combine(field_ref[:REST], field_ref[HALF:], row_parity)
        rows = jnp.concatenate([top, field_ref[REST:HALF]], axis=0)
        folded = []
        for col_parity in (0, 1):
            first = combine(rows[:, :REST], rows[:, HALF:], col_parity)
            folded.append(narrow(jnp.concatenate([first, rows[:, REST:HALF]], axis=1)))
        left.append(narrow(matmul(fwd_ref[row_parity, :, :HALF], jnp.concatenate(folded, axis=1))))
    products = []
    for col_parity in (0, 1):
        tmpl = matmul(side_by_side(left, col_parity), inv_ref[col_parity])
        tmpl_re, tmpl_im = tmpl[:, :HALF], tmpl[:, HALF:]
        image_re, image_im = wide(spec_ref[col_parity, :, :HALF]), wide(spec_ref[col_parity, :, HALF:])
        prod_re = narrow(image_re * tmpl_re + image_im * tmpl_im)
        prod_im = narrow(image_im * tmpl_re - image_re * tmpl_im)
        products.append((prod_re, prod_im))
    left = []
    for row_parity in (0, 1):
        rows = slice(row_parity * HALF, (row_parity + 1) * HALF)
        stacked = [jnp.concatenate([prod_re[rows], prod_im[rows]], axis=0) for prod_re, prod_im in products]
        left.append(narrow(matmul(inv_ref[row_parity], jnp.concatenate(stacked, axis=1))))
    for col_parity in (0, 1):
        back_ref[col_parity] = matmul(side_by_side(left, col_parity), fwd_ref[col_parity])
    rows_out = out_ref.shape[1]
    groups = NP // rows_out
    members = result_members()
    for core in range(CORES):
        cols = slice(core * HALF, (core + 1) * HALF)
        for group in range(groups // 2):
            even = slice(group * rows_out, (group + 1) * rows_out)
            odd = slice(HALF + group * rows_out, HALF + (group + 1) * rows_out)
            even_even, even_odd = back_ref[0, even, cols], back_ref[1, even, cols]
            odd_even, odd_odd = back_ref[0, odd, cols], back_ref[1, odd, cols]
            even_left, odd_left = even_even + even_odd, odd_even + odd_odd
            even_right, odd_right = even_even - even_odd, odd_even - odd_odd
            upper = members.index((group, core))
            lower = members.index((group + groups // 2, core))
            out_ref[upper, :, :HALF] = narrow(even_left + odd_left)
            out_ref[upper, :, HALF:] = narrow(even_right + odd_right)
            out_ref[lower, :, :HALF] = narrow(even_left - odd_left)
            out_ref[lower, :, HALF:] = narrow(even_right - odd_right)


def pairwise(op, values):
    while len(values) > 1:
        values = [op(*values[i : i + 2]) for i in range(0, len(values), 2)]
    return values[0]


def statistics_kernel(values_ref, total_ref, squares_ref, largest_ref):
    scale = 1.0 / (NP * NP)
    count, height, width = values_ref.shape
    for row in range(0, height, 16):
        for col in range(0, width, 128):
            rows, cols = slice(row, row + 16), slice(col, col + 128)
            values = [wide(values_ref[template, rows, cols]) for template in range(count)]
            total_ref[0, rows, cols] = pairwise(jnp.add, values) * jnp.float32(scale)
            squares_ref[0, rows, cols] = pairwise(jnp.add, [v * v for v in values]) * jnp.float32(scale * scale)
            largest_ref[0, rows, cols] = pairwise(jnp.maximum, values) * jnp.float32(scale)


def call(kernel, name, outs, scratch, *operands):
    whole = pl.BlockSpec(memory_space=pltpu.VMEM)
    return pl.pallas_call(
        kernel,
        name=name,
        out_shape=outs,
        in_specs=[whole] * len(operands),
        out_specs=jax.tree.map(lambda _: whole, outs),
        scratch_shapes=scratch,
        compiler_params=pltpu.CompilerParams(vmem_limit_bytes=32 * 1024 * 1024),
    )(*operands)


def plane_place(y, core):
    return (3 * y + 4) % Y * CORES + 1 - core


def column_place(z):
    return 2 * (z % 2) + 1 - z // 2


def plane_members():
    return sorted(((y, c) for y in range(Y) for c in range(CORES)), key=lambda member: plane_place(*member))


def column_members():
    return sorted(range(Z), key=column_place)


def result_members():
    return [(z_lo * 4 + x, c) for x in (2, 3, 0, 1) for c in (1, 0) for z_lo in (1, 0)]


def receive_template(own_template, owners, spec):
    planes = [[(y * Z + z) * CORES + c for y, c in plane_members()] for z in range(Z)]
    columns = [[(y * Z + z) * CORES + c for z in column_members()] for y in range(Y) for c in range(CORES)]
    owner_z = column_place(owners // CORES % Z)
    owner_place = plane_place(owners // (Z * CORES), owners % CORES)
    owner_z, owner_place = (jnp.broadcast_to(place[:, None], (STEPS, M)) for place in (owner_z, owner_place))
    shares = own_template.reshape(PLANE, CHUNK, M)
    shares = lax.all_to_all(shares, "tile", 0, 0, axis_index_groups=planes)
    shares, spec, owner_z, owner_place = lax.optimization_barrier((shares, spec, owner_z, owner_place))
    spread = jax.ShapeDtypeStruct((Z, STEPS, CHUNK, M), jnp.bfloat16)
    shares = call(pick_place_kernel, "pick_place", spread, [], shares, owner_place)
    shares = lax.all_to_all(shares, "tile", 0, 0, axis_index_groups=columns)
    spread = jax.ShapeDtypeStruct((PLANE, CHUNK, M), jnp.bfloat16)
    shares = call(pick_plane_kernel, "pick_plane", spread, [], shares, owner_z)
    return lax.all_to_all(shares, "tile", 0, 0, axis_index_groups=planes), spec


def image_fields(own_tile):
    pairs = [[tile, tile + 1] for tile in range(0, lax.axis_size("tile"), CORES)]
    halves = [lax.all_gather(half, "tile", axis_index_groups=pairs) for half in (own_tile[:HALF], own_tile[HALF:])]
    return halves


def per_device(image_tiles, templates, owners):
    fwd, inv = (jnp.asarray(table) for table in make_tables())
    groups_here = lax.axis_size("orient")
    tiles = lax.axis_size("tile")
    rows_out = NP // groups_here
    spectrum = (2, NP, NP)
    fields = image_fields(image_tiles[0])
    spec = call(image_kernel, "image_spectrum", jax.ShapeDtypeStruct(spectrum, jnp.bfloat16), [], *fields, fwd, inv)
    shares, spec = receive_template(templates[0, 0], owners[0], spec)
    values = call(
        correlate_kernel,
        "correlate",
        jax.ShapeDtypeStruct((groups_here * CORES, rows_out, NP), jnp.bfloat16),
        [pltpu.VMEM((M, M), jnp.float32), pltpu.VMEM(spectrum, jnp.float32)],
        shares,
        spec,
        fwd,
        inv,
    )
    across = [[group * tiles + pair * CORES + c for group, c in result_members()] for pair in range(tiles // CORES)]
    values = lax.all_to_all(values, ("orient", "tile"), 0, 0, axis_index_groups=across)
    out = jax.ShapeDtypeStruct((1, rows_out, NP), jnp.float32)
    return call(statistics_kernel, "statistics", (out, out, out), [], values)


def solution(mesh):
    placed = (P("tile", None, None), P("orient", "tile", None, None), P("orient", None))
    return jax.shard_map(
        per_device,
        mesh=mesh,
        in_specs=placed,
        out_specs=(P("tile", "orient", None), P("tile", "orient", None), P("tile", "orient", None)),
        check_vma=False,
    )
```

```python
import numpy as np
import jax
import jax.numpy as jnp
from jax import lax
from jax.experimental import pallas as pl
from jax.experimental.pallas import tpu as pltpu
from jax.sharding import PartitionSpec as P

STEPS = 2
NP = 512
HALF = NP // 2
M = 384
REST = M - HALF
Y, Z, CORES = 8, 4, 2
PLANE = Y * CORES
CHUNK = M // PLANE


def make_tables():
    line = np.arange(NP)
    phases = (line[:, None] * line[None, :]) % NP
    angles = phases.astype(np.float32) * np.float32(2.0 * 3.141592653589793 / NP)
    cos_table, sin_table = np.cos(angles), np.sin(angles)
    tables = []
    for parity in (0, 1):
        cos_part = cos_table[parity::2, :HALF]
        sin_part = sin_table[parity::2, :HALF]
        tables.append(np.block([[cos_part, sin_part], [-sin_part, cos_part]]))
    tables = np.stack(tables).astype(jnp.bfloat16)
    return tables, np.ascontiguousarray(tables.transpose(0, 2, 1))


def matmul(left, right):
    return jnp.dot(left, right, preferred_element_type=jnp.float32)


def wide(values):
    return values.astype(jnp.float32)


def narrow(values):
    return values.astype(jnp.bfloat16)


def combine(left, right, parity):
    return left + right if parity == 0 else left - right


def pick(shares_ref, place_ref, step):
    total = None
    for place in range(shares_ref.shape[0]):
        share = shares_ref[place, step] if len(shares_ref.shape) == 4 else shares_ref[place]
        here = jnp.where(place_ref[step : step + 1] == place, 1.0, 0.0)
        total = wide(share) * here if total is None else total + wide(share) * here
    return narrow(total)


def pick_place_kernel(shares_ref, place_ref, out_ref):
    for step in range(STEPS):
        share = pick(shares_ref, place_ref, step)
        for receiver in range(out_ref.shape[0]):
            out_ref[receiver, step] = share


def pick_plane_kernel(shares_ref, place_ref, out_ref):
    for step in range(STEPS):
        share = pick(shares_ref, place_ref, step)
        for y in range(Y):
            out_ref[plane_place(y, step)] = share


def side_by_side(left, col_parity):
    cols = slice(col_parity * HALF, (col_parity + 1) * HALF)
    return jnp.concatenate([jnp.concatenate([a[:HALF, cols], a[HALF:, cols]], axis=1) for a in left], axis=0)


def image_kernel(top_ref, low_ref, fwd_ref, inv_ref, spec_ref, level_ref):
    quarters = []
    for core in range(CORES):
        top, low = wide(top_ref[core]), wide(low_ref[core])
        energy = jnp.sum(top * top + low * low, axis=0, keepdims=True)
        energy = jnp.sum(energy, axis=1, keepdims=True)
        level = jnp.where(energy > 0, jnp.sqrt(energy * jnp.float32(1.0 / (NP * NP))), 1.0)
        level = jnp.where(level > 0, level, 1.0)
        level_ref[core : core + 1, :] = jnp.broadcast_to(level, (1, NP))
        top, low = top / level, low / level
        quarters.append((top[:, :HALF], top[:, HALF:], low[:, :HALF], low[:, HALF:]))
    left = []
    for row_parity in (0, 1):
        folded = []
        for col_parity in (0, 1):
            parts = []
            for top_left, top_right, low_left, low_right in quarters:
                left_half = combine(top_left, low_left, row_parity)
                right_half = combine(top_right, low_right, row_parity)
                parts.append(narrow(combine(left_half, right_half, col_parity)))
            folded.append(jnp.concatenate(parts, axis=0))
        left.append(narrow(matmul(fwd_ref[row_parity], jnp.concatenate(folded, axis=1))))
    for col_parity in (0, 1):
        spec_ref[col_parity] = narrow(matmul(side_by_side(left, col_parity), inv_ref[col_parity]))


def correlate_kernel(shares_ref, spec_ref, fwd_ref, inv_ref, out_ref, field_ref, back_ref):
    for place in range(PLANE):
        field_ref[place * CHUNK : (place + 1) * CHUNK, :] = wide(shares_ref[place])
    left = []
    for row_parity in (0, 1):
        top = combine(field_ref[:REST], field_ref[HALF:], row_parity)
        rows = jnp.concatenate([top, field_ref[REST:HALF]], axis=0)
        folded = []
        for col_parity in (0, 1):
            first = combine(rows[:, :REST], rows[:, HALF:], col_parity)
            folded.append(narrow(jnp.concatenate([first, rows[:, REST:HALF]], axis=1)))
        left.append(narrow(matmul(fwd_ref[row_parity, :, :HALF], jnp.concatenate(folded, axis=1))))
    products = []
    for col_parity in (0, 1):
        tmpl = matmul(side_by_side(left, col_parity), inv_ref[col_parity])
        tmpl_re, tmpl_im = tmpl[:, :HALF], tmpl[:, HALF:]
        image_re, image_im = wide(spec_ref[col_parity, :, :HALF]), wide(spec_ref[col_parity, :, HALF:])
        prod_re = narrow(image_re * tmpl_re + image_im * tmpl_im)
        prod_im = narrow(image_im * tmpl_re - image_re * tmpl_im)
        products.append((prod_re, prod_im))
    left = []
    for row_parity in (0, 1):
        rows = slice(row_parity * HALF, (row_parity + 1) * HALF)
        stacked = [jnp.concatenate([prod_re[rows], prod_im[rows]], axis=0) for prod_re, prod_im in products]
        left.append(narrow(matmul(inv_ref[row_parity], jnp.concatenate(stacked, axis=1))))
    for col_parity in (0, 1):
        back_ref[col_parity] = matmul(side_by_side(left, col_parity), fwd_ref[col_parity])
    rows_out = out_ref.shape[1]
    groups = NP // rows_out
    members = result_members()
    for core in range(CORES):
        cols = slice(core * HALF, (core + 1) * HALF)
        for group in range(groups // 2):
            even = slice(group * rows_out, (group + 1) * rows_out)
            odd = slice(HALF + group * rows_out, HALF + (group + 1) * rows_out)
            even_even, even_odd = back_ref[0, even, cols], back_ref[1, even, cols]
            odd_even, odd_odd = back_ref[0, odd, cols], back_ref[1, odd, cols]
            even_left, odd_left = even_even + even_odd, odd_even + odd_odd
            even_right, odd_right = even_even - even_odd, odd_even - odd_odd
            upper = members.index((group, core))
            lower = members.index((group + groups // 2, core))
            out_ref[upper, :, :HALF] = narrow(even_left + odd_left)
            out_ref[upper, :, HALF:] = narrow(even_right + odd_right)
            out_ref[lower, :, :HALF] = narrow(even_left - odd_left)
            out_ref[lower, :, HALF:] = narrow(even_right - odd_right)


def pairwise(op, values):
    while len(values) > 1:
        values = [op(*values[i : i + 2]) for i in range(0, len(values), 2)]
    return values[0]


def statistics_kernel(values_ref, level_ref, total_ref, squares_ref, largest_ref):
    scale = level_ref[...] * jnp.float32(1.0 / (NP * NP))
    count, height, width = values_ref.shape
    for row in range(0, height, 16):
        for col in range(0, width, 128):
            rows, cols = slice(row, row + 16), slice(col, col + 128)
            values = [wide(values_ref[template, rows, cols]) for template in range(count)]
            total_ref[0, rows, cols] = pairwise(jnp.add, values) * scale[:, cols]
            squares_ref[0, rows, cols] = pairwise(jnp.add, [v * v for v in values]) * (scale * scale)[:, cols]
            largest_ref[0, rows, cols] = pairwise(jnp.maximum, values) * scale[:, cols]


def call(kernel, name, outs, scratch, *operands):
    whole = pl.BlockSpec(memory_space=pltpu.VMEM)
    return pl.pallas_call(
        kernel,
        name=name,
        out_shape=outs,
        in_specs=[whole] * len(operands),
        out_specs=jax.tree.map(lambda _: whole, outs),
        scratch_shapes=scratch,
        compiler_params=pltpu.CompilerParams(vmem_limit_bytes=32 * 1024 * 1024),
    )(*operands)


def plane_place(y, core):
    return (3 * y + 4) % Y * CORES + 1 - core


def column_place(z):
    return 2 * (z % 2) + 1 - z // 2


def plane_members():
    return sorted(((y, c) for y in range(Y) for c in range(CORES)), key=lambda member: plane_place(*member))


def column_members():
    return sorted(range(Z), key=column_place)


def result_members():
    return [(z_lo * 4 + x, c) for x in (2, 3, 0, 1) for c in (1, 0) for z_lo in (1, 0)]


def receive_template(own_template, owners, spec, own_level):
    planes = [[(y * Z + z) * CORES + c for y, c in plane_members()] for z in range(Z)]
    columns = [[(y * Z + z) * CORES + c for z in column_members()] for y in range(Y) for c in range(CORES)]
    owner_z = column_place(owners // CORES % Z)
    owner_place = plane_place(owners // (Z * CORES), owners % CORES)
    owner_z, owner_place = (jnp.broadcast_to(place[:, None], (STEPS, M)) for place in (owner_z, owner_place))
    shares = own_template.reshape(PLANE, CHUNK, M)
    shares = lax.all_to_all(shares, "tile", 0, 0, axis_index_groups=planes)
    shares, spec, own_level, owner_z, owner_place = lax.optimization_barrier(
        (shares, spec, own_level, owner_z, owner_place)
    )
    spread = jax.ShapeDtypeStruct((Z, STEPS, CHUNK, M), jnp.bfloat16)
    shares = call(pick_place_kernel, "pick_place", spread, [], shares, owner_place)
    shares = lax.all_to_all(shares, "tile", 0, 0, axis_index_groups=columns)
    spread = jax.ShapeDtypeStruct((PLANE, CHUNK, M), jnp.bfloat16)
    shares = call(pick_plane_kernel, "pick_plane", spread, [], shares, owner_z)
    return lax.all_to_all(shares, "tile", 0, 0, axis_index_groups=planes), spec, own_level


def image_fields(own_tile):
    pairs = [[tile, tile + 1] for tile in range(0, lax.axis_size("tile"), CORES)]
    halves = [lax.all_gather(half, "tile", axis_index_groups=pairs) for half in (own_tile[:HALF], own_tile[HALF:])]
    return halves


def per_device(image_tiles, templates, owners):
    fwd, inv = (jnp.asarray(table) for table in make_tables())
    groups_here = lax.axis_size("orient")
    tiles = lax.axis_size("tile")
    rows_out = NP // groups_here
    spectrum = (2, NP, NP)
    fields = image_fields(image_tiles[0])
    image_outs = (jax.ShapeDtypeStruct(spectrum, jnp.bfloat16), jax.ShapeDtypeStruct((CORES, NP), jnp.float32))
    spec, levels = call(image_kernel, "image_spectrum", image_outs, [], *fields, fwd, inv)
    own_level = jnp.where(lax.axis_index("tile") % CORES == 0, levels[:1], levels[1:])
    shares, spec, own_level = receive_template(templates[0, 0], owners[0], spec, own_level)
    values = call(
        correlate_kernel,
        "correlate",
        jax.ShapeDtypeStruct((groups_here * CORES, rows_out, NP), jnp.bfloat16),
        [pltpu.VMEM((M, M), jnp.float32), pltpu.VMEM(spectrum, jnp.float32)],
        shares,
        spec,
        fwd,
        inv,
    )
    across = [[group * tiles + pair * CORES + c for group, c in result_members()] for pair in range(tiles // CORES)]
    values = lax.all_to_all(values, ("orient", "tile"), 0, 0, axis_index_groups=across)
    out = jax.ShapeDtypeStruct((1, rows_out, NP), jnp.float32)
    return call(statistics_kernel, "statistics", (out, out, out), [], values, own_level)


def solution(mesh):
    placed = (P("tile", None, None), P("orient", "tile", None, None), P("orient", None))
    return jax.shard_map(
        per_device,
        mesh=mesh,
        in_specs=placed,
        out_specs=(P("tile", "orient", None), P("tile", "orient", None), P("tile", "orient", None)),
        check_vma=False,
    )
```

```python
import numpy as np
import jax
import jax.numpy as jnp
from jax import lax
from jax.experimental import pallas as pl
from jax.experimental.pallas import tpu as pltpu
from jax.sharding import PartitionSpec as P

STEPS = 2
NP = 512
HALF = NP // 2
M = 384
REST = M - HALF
Y, Z, CORES = 8, 4, 2
PLANE = Y * CORES
CHUNK = M // PLANE


def make_tables():
    line = np.arange(NP)
    phases = (line[:, None] * line[None, :]) % NP
    angles = phases.astype(np.float32) * np.float32(2.0 * 3.141592653589793 / NP)
    cos_table, sin_table = np.cos(angles), np.sin(angles)
    tables = []
    for parity in (0, 1):
        cos_part = cos_table[parity::2, :HALF]
        sin_part = sin_table[parity::2, :HALF]
        tables.append(np.block([[cos_part, sin_part], [-sin_part, cos_part]]))
    tables = np.stack(tables).astype(jnp.bfloat16)
    return tables, np.ascontiguousarray(tables.transpose(0, 2, 1))


def matmul(left, right):
    return jnp.dot(left, right, preferred_element_type=jnp.float32)


def wide(values):
    return values.astype(jnp.float32)


def narrow(values):
    return values.astype(jnp.bfloat16)


def combine(left, right, parity):
    return left + right if parity == 0 else left - right


def pick(shares_ref, place_ref, step):
    total = None
    for place in range(shares_ref.shape[0]):
        share = shares_ref[place, step] if len(shares_ref.shape) == 4 else shares_ref[place]
        here = jnp.where(place_ref[step : step + 1] == place, 1.0, 0.0)
        total = wide(share) * here if total is None else total + wide(share) * here
    return narrow(total)


def pick_place_kernel(shares_ref, place_ref, out_ref):
    for step in range(STEPS):
        share = pick(shares_ref, place_ref, step)
        for receiver in range(out_ref.shape[0]):
            out_ref[receiver, step] = share


def pick_plane_kernel(shares_ref, place_ref, out_ref):
    for step in range(STEPS):
        share = pick(shares_ref, place_ref, step)
        for y in range(Y):
            out_ref[plane_place(y, step)] = share


def side_by_side(left, col_parity):
    cols = slice(col_parity * HALF, (col_parity + 1) * HALF)
    return jnp.concatenate([jnp.concatenate([a[:HALF, cols], a[HALF:, cols]], axis=1) for a in left], axis=0)


def image_kernel(top_ref, low_ref, fwd_ref, inv_ref, spec_ref, level_ref):
    quarters = []
    for core in range(CORES):
        top, low = wide(top_ref[core]), wide(low_ref[core])
        energy = jnp.sum(top * top + low * low, axis=0, keepdims=True)
        energy = jnp.sum(energy, axis=1, keepdims=True)
        level = jnp.where(energy > 0, jnp.sqrt(energy * jnp.float32(1.0 / (NP * NP))), 1.0)
        level = jnp.where(level > 0, level, 1.0)
        level_ref[core : core + 1, :] = jnp.broadcast_to(level, (1, NP))
        top, low = top / level, low / level
        quarters.append((top[:, :HALF], top[:, HALF:], low[:, :HALF], low[:, HALF:]))
    left = []
    for row_parity in (0, 1):
        folded = []
        for col_parity in (0, 1):
            parts = []
            for top_left, top_right, low_left, low_right in quarters:
                left_half = combine(top_left, low_left, row_parity)
                right_half = combine(top_right, low_right, row_parity)
                parts.append(narrow(combine(left_half, right_half, col_parity)))
            folded.append(jnp.concatenate(parts, axis=0))
        left.append(narrow(matmul(fwd_ref[row_parity], jnp.concatenate(folded, axis=1))))
    for col_parity in (0, 1):
        spec_ref[col_parity] = narrow(matmul(side_by_side(left, col_parity), inv_ref[col_parity]))


def correlate_kernel(shares_ref, spec_ref, fwd_ref, inv_ref, out_ref, back_ref):
    field = jnp.concatenate([wide(shares_ref[place]) for place in range(PLANE)], axis=0)
    left = []
    for row_parity in (0, 1):
        top = combine(field[:REST], field[HALF:], row_parity)
        rows = jnp.concatenate([top, field[REST:HALF]], axis=0)
        folded = []
        for col_parity in (0, 1):
            first = combine(rows[:, :REST], rows[:, HALF:], col_parity)
            folded.append(narrow(jnp.concatenate([first, rows[:, REST:HALF]], axis=1)))
        left.append(narrow(matmul(fwd_ref[row_parity, :, :HALF], jnp.concatenate(folded, axis=1))))
    products = []
    for col_parity in (0, 1):
        tmpl = matmul(side_by_side(left, col_parity), inv_ref[col_parity])
        tmpl_re, tmpl_im = tmpl[:, :HALF], tmpl[:, HALF:]
        image_re, image_im = wide(spec_ref[col_parity, :, :HALF]), wide(spec_ref[col_parity, :, HALF:])
        prod_re = narrow(image_re * tmpl_re + image_im * tmpl_im)
        prod_im = narrow(image_im * tmpl_re - image_re * tmpl_im)
        products.append((prod_re, prod_im))
    left = []
    for row_parity in (0, 1):
        rows = slice(row_parity * HALF, (row_parity + 1) * HALF)
        stacked = [jnp.concatenate([prod_re[rows], prod_im[rows]], axis=0) for prod_re, prod_im in products]
        left.append(narrow(matmul(inv_ref[row_parity], jnp.concatenate(stacked, axis=1))))
    for col_parity in (0, 1):
        back_ref[col_parity] = matmul(side_by_side(left, col_parity), fwd_ref[col_parity])
    rows_out = out_ref.shape[1]
    groups = NP // rows_out
    members = result_members()
    for core in range(CORES):
        cols = slice(core * HALF, (core + 1) * HALF)
        for group in range(groups // 2):
            even = slice(group * rows_out, (group + 1) * rows_out)
            odd = slice(HALF + group * rows_out, HALF + (group + 1) * rows_out)
            even_even, even_odd = back_ref[0, even, cols], back_ref[1, even, cols]
            odd_even, odd_odd = back_ref[0, odd, cols], back_ref[1, odd, cols]
            even_left, odd_left = even_even + even_odd, odd_even + odd_odd
            even_right, odd_right = even_even - even_odd, odd_even - odd_odd
            upper = members.index((group, core))
            lower = members.index((group + groups // 2, core))
            out_ref[upper, :, :HALF] = narrow(even_left + odd_left)
            out_ref[upper, :, HALF:] = narrow(even_right + odd_right)
            out_ref[lower, :, :HALF] = narrow(even_left - odd_left)
            out_ref[lower, :, HALF:] = narrow(even_right - odd_right)


def pairwise(op, values):
    while len(values) > 1:
        values = [op(*values[i : i + 2]) for i in range(0, len(values), 2)]
    return values[0]


def statistics_kernel(values_ref, level_ref, total_ref, squares_ref, largest_ref):
    scale = level_ref[...] * jnp.float32(1.0 / (NP * NP))
    count, height, width = values_ref.shape
    for row in range(0, height, 16):
        for col in range(0, width, 128):
            rows, cols = slice(row, row + 16), slice(col, col + 128)
            values = [wide(values_ref[template, rows, cols]) for template in range(count)]
            total_ref[0, rows, cols] = pairwise(jnp.add, values) * scale[:, cols]
            squares_ref[0, rows, cols] = pairwise(jnp.add, [v * v for v in values]) * (scale * scale)[:, cols]
            largest_ref[0, rows, cols] = pairwise(jnp.maximum, values) * scale[:, cols]


def call(kernel, name, outs, scratch, *operands):
    whole = pl.BlockSpec(memory_space=pltpu.VMEM)
    return pl.pallas_call(
        kernel,
        name=name,
        out_shape=outs,
        in_specs=[whole] * len(operands),
        out_specs=jax.tree.map(lambda _: whole, outs),
        scratch_shapes=scratch,
        compiler_params=pltpu.CompilerParams(vmem_limit_bytes=32 * 1024 * 1024),
    )(*operands)


def plane_place(y, core):
    return (3 * y + 4) % Y * CORES + 1 - core


def column_place(z):
    return 2 * (z % 2) + 1 - z // 2


def plane_members():
    return sorted(((y, c) for y in range(Y) for c in range(CORES)), key=lambda member: plane_place(*member))


def column_members():
    return sorted(range(Z), key=column_place)


def result_members():
    return [(z_lo * 4 + x, c) for x in (2, 3, 0, 1) for c in (1, 0) for z_lo in (1, 0)]


def receive_template(own_template, owners, spec, own_level):
    planes = [[(y * Z + z) * CORES + c for y, c in plane_members()] for z in range(Z)]
    columns = [[(y * Z + z) * CORES + c for z in column_members()] for y in range(Y) for c in range(CORES)]
    owner_z = column_place(owners // CORES % Z)
    owner_place = plane_place(owners // (Z * CORES), owners % CORES)
    owner_z, owner_place = owner_z[:, None], owner_place[:, None]
    shares = own_template.reshape(PLANE, CHUNK, M)
    shares = lax.all_to_all(shares, "tile", 0, 0, axis_index_groups=planes)
    shares, spec, own_level, owner_z, owner_place = lax.optimization_barrier(
        (shares, spec, own_level, owner_z, owner_place)
    )
    spread = jax.ShapeDtypeStruct((Z, STEPS, CHUNK, M), jnp.bfloat16)
    shares = call(pick_place_kernel, "pick_place", spread, [], shares, owner_place)
    shares = lax.all_to_all(shares, "tile", 0, 0, axis_index_groups=columns)
    spread = jax.ShapeDtypeStruct((PLANE, CHUNK, M), jnp.bfloat16)
    shares = call(pick_plane_kernel, "pick_plane", spread, [], shares, owner_z)
    return lax.all_to_all(shares, "tile", 0, 0, axis_index_groups=planes), spec, own_level


def image_fields(own_tile):
    pairs = [[tile, tile + 1] for tile in range(0, lax.axis_size("tile"), CORES)]
    halves = [lax.all_gather(half, "tile", axis_index_groups=pairs) for half in (own_tile[:HALF], own_tile[HALF:])]
    return halves


def per_device(image_tiles, templates, owners):
    fwd, inv = (jnp.asarray(table) for table in make_tables())
    groups_here = lax.axis_size("orient")
    tiles = lax.axis_size("tile")
    rows_out = NP // groups_here
    spectrum = (2, NP, NP)
    fields = image_fields(image_tiles[0])
    image_outs = (jax.ShapeDtypeStruct(spectrum, jnp.bfloat16), jax.ShapeDtypeStruct((CORES, NP), jnp.float32))
    spec, levels = call(image_kernel, "image_spectrum", image_outs, [], *fields, fwd, inv)
    own_level = jnp.where(lax.axis_index("tile") % CORES == 0, levels[:1], levels[1:])
    shares, spec, own_level = receive_template(templates[0, 0], owners[0], spec, own_level)
    values = call(
        correlate_kernel,
        "correlate",
        jax.ShapeDtypeStruct((groups_here * CORES, rows_out, NP), jnp.bfloat16),
        [pltpu.VMEM(spectrum, jnp.float32)],
        shares,
        spec,
        fwd,
        inv,
    )
    across = [[group * tiles + pair * CORES + c for group, c in result_members()] for pair in range(tiles // CORES)]
    values = lax.all_to_all(values, ("orient", "tile"), 0, 0, axis_index_groups=across)
    out = jax.ShapeDtypeStruct((1, rows_out, NP), jnp.float32)
    return call(statistics_kernel, "statistics", (out, out, out), [], values, own_level)


def solution(mesh):
    placed = (P("tile", None, None), P("orient", "tile", None, None), P("orient", None))
    return jax.shard_map(
        per_device,
        mesh=mesh,
        in_specs=placed,
        out_specs=(P("tile", "orient", None), P("tile", "orient", None), P("tile", "orient", None)),
        check_vma=False,
    )
```

```python
import numpy as np
import jax
import jax.numpy as jnp
from jax import lax
from jax.experimental import pallas as pl
from jax.experimental.pallas import tpu as pltpu
from jax.sharding import PartitionSpec as P

STEPS = 2
NP = 512
HALF = NP // 2
M = 384
REST = M - HALF
Y, Z, CORES = 8, 4, 2
PLANE = Y * CORES
CHUNK = M // PLANE


def make_tables():
    line = np.arange(NP)
    phases = (line[:, None] * line[None, :]) % NP
    angles = phases.astype(np.float32) * np.float32(2.0 * 3.141592653589793 / NP)
    cos_table, sin_table = np.cos(angles), np.sin(angles)
    tables = []
    for parity in (0, 1):
        cos_part = cos_table[parity::2, :HALF]
        sin_part = sin_table[parity::2, :HALF]
        tables.append(np.block([[cos_part, sin_part], [-sin_part, cos_part]]))
    tables = np.stack(tables).astype(jnp.bfloat16)
    return tables, np.ascontiguousarray(tables.transpose(0, 2, 1))


def matmul(left, right):
    return jnp.dot(left, right, preferred_element_type=jnp.float32)


def wide(values):
    return values.astype(jnp.float32)


def narrow(values):
    return values.astype(jnp.bfloat16)


def combine(left, right, parity):
    return left + right if parity == 0 else left - right


def pick(shares_ref, place_ref, step):
    total = None
    for place in range(shares_ref.shape[0]):
        share = shares_ref[place, step] if len(shares_ref.shape) == 4 else shares_ref[place]
        here = jnp.where(place_ref[step : step + 1] == place, 1.0, 0.0)
        total = wide(share) * here if total is None else total + wide(share) * here
    return narrow(total)


def pick_kernel(shares_ref, place_ref, out_ref):
    for step in range(STEPS):
        out_ref[step] = pick(shares_ref, place_ref, step)


def pick_plane_kernel(shares_ref, place_ref, out_ref):
    for step in range(STEPS):
        share = pick(shares_ref, place_ref, step)
        for y in range(Y):
            out_ref[plane_place(y, step)] = share


def side_by_side(left, col_parity):
    cols = slice(col_parity * HALF, (col_parity + 1) * HALF)
    return jnp.concatenate([jnp.concatenate([a[:HALF, cols], a[HALF:, cols]], axis=1) for a in left], axis=0)


def image_kernel(top_ref, low_ref, fwd_ref, inv_ref, spec_ref, level_ref):
    quarters = []
    for core in range(CORES):
        top, low = wide(top_ref[core]), wide(low_ref[core])
        energy = jnp.sum(top * top + low * low, axis=0, keepdims=True)
        energy = jnp.sum(energy, axis=1, keepdims=True)
        level = jnp.where(energy > 0, jnp.sqrt(energy * jnp.float32(1.0 / (NP * NP))), 1.0)
        level = jnp.where(level > 0, level, 1.0)
        level_ref[core : core + 1, :] = jnp.broadcast_to(level, (1, NP))
        top, low = top / level, low / level
        quarters.append((top[:, :HALF], top[:, HALF:], low[:, :HALF], low[:, HALF:]))
    left = []
    for row_parity in (0, 1):
        folded = []
        for col_parity in (0, 1):
            parts = []
            for top_left, top_right, low_left, low_right in quarters:
                left_half = combine(top_left, low_left, row_parity)
                right_half = combine(top_right, low_right, row_parity)
                parts.append(narrow(combine(left_half, right_half, col_parity)))
            folded.append(jnp.concatenate(parts, axis=0))
        left.append(narrow(matmul(fwd_ref[row_parity], jnp.concatenate(folded, axis=1))))
    for col_parity in (0, 1):
        spec_ref[col_parity] = narrow(matmul(side_by_side(left, col_parity), inv_ref[col_parity]))


def correlate_kernel(shares_ref, spec_ref, fwd_ref, inv_ref, out_ref, field_ref, back_ref):
    for place in range(PLANE):
        field_ref[place * CHUNK : (place + 1) * CHUNK, :] = wide(shares_ref[place])
    left = []
    for row_parity in (0, 1):
        top = combine(field_ref[:REST], field_ref[HALF:], row_parity)
        rows = jnp.concatenate([top, field_ref[REST:HALF]], axis=0)
        folded = []
        for col_parity in (0, 1):
            first = combine(rows[:, :REST], rows[:, HALF:], col_parity)
            folded.append(narrow(jnp.concatenate([first, rows[:, REST:HALF]], axis=1)))
        left.append(narrow(matmul(fwd_ref[row_parity, :, :HALF], jnp.concatenate(folded, axis=1))))
    products = []
    for col_parity in (0, 1):
        tmpl = matmul(side_by_side(left, col_parity), inv_ref[col_parity])
        tmpl_re, tmpl_im = tmpl[:, :HALF], tmpl[:, HALF:]
        image_re, image_im = wide(spec_ref[col_parity, :, :HALF]), wide(spec_ref[col_parity, :, HALF:])
        prod_re = narrow(image_re * tmpl_re + image_im * tmpl_im)
        prod_im = narrow(image_im * tmpl_re - image_re * tmpl_im)
        products.append((prod_re, prod_im))
    left = []
    for row_parity in (0, 1):
        rows = slice(row_parity * HALF, (row_parity + 1) * HALF)
        stacked = [jnp.concatenate([prod_re[rows], prod_im[rows]], axis=0) for prod_re, prod_im in products]
        left.append(narrow(matmul(inv_ref[row_parity], jnp.concatenate(stacked, axis=1))))
    for col_parity in (0, 1):
        back_ref[col_parity] = matmul(side_by_side(left, col_parity), fwd_ref[col_parity])
    rows_out = out_ref.shape[1]
    groups = NP // rows_out
    members = result_members()
    for core in range(CORES):
        cols = slice(core * HALF, (core + 1) * HALF)
        for group in range(groups // 2):
            even = slice(group * rows_out, (group + 1) * rows_out)
            odd = slice(HALF + group * rows_out, HALF + (group + 1) * rows_out)
            even_even, even_odd = back_ref[0, even, cols], back_ref[1, even, cols]
            odd_even, odd_odd = back_ref[0, odd, cols], back_ref[1, odd, cols]
            even_left, odd_left = even_even + even_odd, odd_even + odd_odd
            even_right, odd_right = even_even - even_odd, odd_even - odd_odd
            upper = members.index((group, core))
            lower = members.index((group + groups // 2, core))
            out_ref[upper, :, :HALF] = narrow(even_left + odd_left)
            out_ref[upper, :, HALF:] = narrow(even_right + odd_right)
            out_ref[lower, :, :HALF] = narrow(even_left - odd_left)
            out_ref[lower, :, HALF:] = narrow(even_right - odd_right)


def pairwise(op, values):
    while len(values) > 1:
        values = [op(*values[i : i + 2]) for i in range(0, len(values), 2)]
    return values[0]


def statistics_kernel(values_ref, level_ref, total_ref, squares_ref, largest_ref):
    scale = level_ref[...] * jnp.float32(1.0 / (NP * NP))
    count, height, width = values_ref.shape
    for row in range(0, height, 16):
        for col in range(0, width, 128):
            rows, cols = slice(row, row + 16), slice(col, col + 128)
            values = [wide(values_ref[template, rows, cols]) for template in range(count)]
            total_ref[0, rows, cols] = pairwise(jnp.add, values) * scale[:, cols]
            squares_ref[0, rows, cols] = pairwise(jnp.add, [v * v for v in values]) * (scale * scale)[:, cols]
            largest_ref[0, rows, cols] = pairwise(jnp.maximum, values) * scale[:, cols]


def call(kernel, name, outs, scratch, *operands):
    whole = pl.BlockSpec(memory_space=pltpu.VMEM)
    return pl.pallas_call(
        kernel,
        name=name,
        out_shape=outs,
        in_specs=[whole] * len(operands),
        out_specs=jax.tree.map(lambda _: whole, outs),
        scratch_shapes=scratch,
        compiler_params=pltpu.CompilerParams(vmem_limit_bytes=32 * 1024 * 1024),
    )(*operands)


def plane_place(y, core):
    return (3 * y + 4) % Y * CORES + 1 - core


def plane_members():
    return sorted(((y, c) for y in range(Y) for c in range(CORES)), key=lambda member: plane_place(*member))


def z_pairs(pairs):
    return [[(y * Z + z) * CORES + c for z in pair] for pair in pairs for y in range(Y) for c in range(CORES)]


def result_members():
    return [(z_lo * 4 + x, c) for x in (2, 3, 0, 1) for c in (1, 0) for z_lo in (1, 0)]


def receive_template(own_template, owners, spec, own_level):
    planes = [[(y * Z + z) * CORES + c for y, c in plane_members()] for z in range(Z)]
    owner_z = owners // CORES % Z
    owner_place = plane_place(owners // (Z * CORES), owners % CORES)
    owner_place, owner_near, owner_far = (
        jnp.broadcast_to(place[:, None], (STEPS, M)) for place in (owner_place, owner_z % 2, owner_z // 2)
    )
    shares = own_template.reshape(PLANE, CHUNK, M)
    shares = lax.all_to_all(shares, "tile", 0, 0, axis_index_groups=planes)
    shares, spec, own_level, owner_place, owner_near, owner_far = lax.optimization_barrier(
        (shares, spec, own_level, owner_place, owner_near, owner_far)
    )
    kept = jax.ShapeDtypeStruct((STEPS, CHUNK, M), jnp.bfloat16)
    shares = call(pick_kernel, "pick_place", kept, [], shares, owner_place)
    shares = lax.all_gather(shares, "tile", axis_index_groups=z_pairs(((0, 1), (2, 3))))
    shares = call(pick_kernel, "pick_near", kept, [], shares, owner_near)
    shares = lax.all_gather(shares, "tile", axis_index_groups=z_pairs(((0, 3), (1, 2))))
    spread = jax.ShapeDtypeStruct((PLANE, CHUNK, M), jnp.bfloat16)
    shares = call(pick_plane_kernel, "pick_far", spread, [], shares, owner_far)
    return lax.all_to_all(shares, "tile", 0, 0, axis_index_groups=planes), spec, own_level


def image_fields(own_tile):
    pairs = [[tile, tile + 1] for tile in range(0, lax.axis_size("tile"), CORES)]
    halves = [lax.all_gather(half, "tile", axis_index_groups=pairs) for half in (own_tile[:HALF], own_tile[HALF:])]
    return halves


def per_device(image_tiles, templates, owners):
    fwd, inv = (jnp.asarray(table) for table in make_tables())
    groups_here = lax.axis_size("orient")
    tiles = lax.axis_size("tile")
    rows_out = NP // groups_here
    spectrum = (2, NP, NP)
    fields = image_fields(image_tiles[0])
    image_outs = (jax.ShapeDtypeStruct(spectrum, jnp.bfloat16), jax.ShapeDtypeStruct((CORES, NP), jnp.float32))
    spec, levels = call(image_kernel, "image_spectrum", image_outs, [], *fields, fwd, inv)
    own_level = jnp.where(lax.axis_index("tile") % CORES == 0, levels[:1], levels[1:])
    shares, spec, own_level = receive_template(templates[0, 0], owners[0], spec, own_level)
    values = call(
        correlate_kernel,
        "correlate",
        jax.ShapeDtypeStruct((groups_here * CORES, rows_out, NP), jnp.bfloat16),
        [pltpu.VMEM((M, M), jnp.float32), pltpu.VMEM(spectrum, jnp.float32)],
        shares,
        spec,
        fwd,
        inv,
    )
    across = [[group * tiles + pair * CORES + c for group, c in result_members()] for pair in range(tiles // CORES)]
    values = lax.all_to_all(values, ("orient", "tile"), 0, 0, axis_index_groups=across)
    out = jax.ShapeDtypeStruct((1, rows_out, NP), jnp.float32)
    return call(statistics_kernel, "statistics", (out, out, out), [], values, own_level)


def solution(mesh):
    placed = (P("tile", None, None), P("orient", "tile", None, None), P("orient", None))
    return jax.shard_map(
        per_device,
        mesh=mesh,
        in_specs=placed,
        out_specs=(P("tile", "orient", None), P("tile", "orient", None), P("tile", "orient", None)),
        check_vma=False,
    )
```

```python
import numpy as np
import jax
import jax.numpy as jnp
from jax import lax
from jax.experimental import pallas as pl
from jax.experimental.pallas import tpu as pltpu
from jax.sharding import PartitionSpec as P

STEPS = 2
NP = 512
HALF = NP // 2
M = 384
REST = M - HALF
Y, Z, CORES = 8, 4, 2
PLANE = Y * CORES
CHUNK = M // PLANE


def make_tables():
    line = np.arange(NP)
    phases = (line[:, None] * line[None, :]) % NP
    angles = phases.astype(np.float32) * np.float32(2.0 * 3.141592653589793 / NP)
    cos_table, sin_table = np.cos(angles), np.sin(angles)
    tables = []
    for parity in (0, 1):
        cos_part = cos_table[parity::2, :HALF]
        sin_part = sin_table[parity::2, :HALF]
        tables.append(np.block([[cos_part, sin_part], [-sin_part, cos_part]]))
    tables = np.stack(tables).astype(jnp.bfloat16)
    return tables, np.ascontiguousarray(tables.transpose(0, 2, 1))


def matmul(left, right):
    return jnp.dot(left, right, preferred_element_type=jnp.float32)


def wide(values):
    return values.astype(jnp.float32)


def narrow(values):
    return values.astype(jnp.bfloat16)


def combine(left, right, parity):
    return left + right if parity == 0 else left - right


def pick(shares_ref, place_ref, step):
    total = None
    for place in range(shares_ref.shape[0]):
        share = shares_ref[place, step] if len(shares_ref.shape) == 4 else shares_ref[place]
        here = jnp.where(place_ref[step : step + 1] == place, 1.0, 0.0)
        total = wide(share) * here if total is None else total + wide(share) * here
    return narrow(total)


def pick_place_kernel(shares_ref, place_ref, out_ref):
    for step in range(STEPS):
        share = pick(shares_ref, place_ref, step)
        for receiver in range(out_ref.shape[0]):
            out_ref[receiver, step] = share


def pick_plane_kernel(shares_ref, place_ref, out_ref):
    for step in range(STEPS):
        share = pick(shares_ref, place_ref, step)
        for y in range(Y):
            out_ref[plane_place(y, step)] = share


def side_by_side(left, col_parity):
    cols = slice(col_parity * HALF, (col_parity + 1) * HALF)
    return jnp.concatenate([jnp.concatenate([a[:HALF, cols], a[HALF:, cols]], axis=1) for a in left], axis=0)


def image_kernel(top_ref, low_ref, fwd_ref, inv_ref, spec_ref, level_ref):
    quarters = []
    for core in range(CORES):
        top, low = wide(top_ref[core]), wide(low_ref[core])
        energy = jnp.sum(top * top + low * low, axis=0, keepdims=True)
        energy = jnp.sum(energy, axis=1, keepdims=True)
        level = jnp.where(energy > 0, jnp.sqrt(energy * jnp.float32(1.0 / (NP * NP))), 1.0)
        level = jnp.where(level > 0, level, 1.0)
        level_ref[core : core + 1, :] = jnp.broadcast_to(level, (1, NP))
        top, low = top / level, low / level
        quarters.append((top[:, :HALF], top[:, HALF:], low[:, :HALF], low[:, HALF:]))
    left = []
    for row_parity in (0, 1):
        folded = []
        for col_parity in (0, 1):
            parts = []
            for top_left, top_right, low_left, low_right in quarters:
                left_half = combine(top_left, low_left, row_parity)
                right_half = combine(top_right, low_right, row_parity)
                parts.append(narrow(combine(left_half, right_half, col_parity)))
            folded.append(jnp.concatenate(parts, axis=0))
        left.append(narrow(matmul(fwd_ref[row_parity], jnp.concatenate(folded, axis=1))))
    for col_parity in (0, 1):
        spec_ref[col_parity] = narrow(matmul(side_by_side(left, col_parity), inv_ref[col_parity]))


def correlate_kernel(shares_ref, spec_ref, fwd_ref, inv_ref, out_ref, field_ref, back_ref):
    for place in range(PLANE):
        field_ref[place * CHUNK : (place + 1) * CHUNK, :] = wide(shares_ref[place])
    left = []
    for row_parity in (0, 1):
        top = combine(field_ref[:REST], field_ref[HALF:], row_parity)
        rows = jnp.concatenate([top, field_ref[REST:HALF]], axis=0)
        folded = []
        for col_parity in (0, 1):
            first = combine(rows[:, :REST], rows[:, HALF:], col_parity)
            folded.append(narrow(jnp.concatenate([first, rows[:, REST:HALF]], axis=1)))
        left.append(narrow(matmul(fwd_ref[row_parity, :, :HALF], jnp.concatenate(folded, axis=1))))
    products = []
    for col_parity in (0, 1):
        tmpl = matmul(side_by_side(left, col_parity), inv_ref[col_parity])
        tmpl_re, tmpl_im = tmpl[:, :HALF], tmpl[:, HALF:]
        image_re, image_im = wide(spec_ref[col_parity, :, :HALF]), wide(spec_ref[col_parity, :, HALF:])
        prod_re = narrow(image_re * tmpl_re + image_im * tmpl_im)
        prod_im = narrow(image_im * tmpl_re - image_re * tmpl_im)
        products.append((prod_re, prod_im))
    left = []
    for row_parity in (0, 1):
        rows = slice(row_parity * HALF, (row_parity + 1) * HALF)
        stacked = [jnp.concatenate([prod_re[rows], prod_im[rows]], axis=0) for prod_re, prod_im in products]
        left.append(narrow(matmul(inv_ref[row_parity], jnp.concatenate(stacked, axis=1))))
    for col_parity in (0, 1):
        back_ref[col_parity] = matmul(side_by_side(left, col_parity), fwd_ref[col_parity])
    rows_out = out_ref.shape[1]
    groups = NP // rows_out
    members = result_members()
    for core in range(CORES):
        cols = slice(core * HALF, (core + 1) * HALF)
        for group in range(groups // 2):
            even = slice(group * rows_out, (group + 1) * rows_out)
            odd = slice(HALF + group * rows_out, HALF + (group + 1) * rows_out)
            even_even, even_odd = back_ref[0, even, cols], back_ref[1, even, cols]
            odd_even, odd_odd = back_ref[0, odd, cols], back_ref[1, odd, cols]
            even_left, odd_left = even_even + even_odd, odd_even + odd_odd
            even_right, odd_right = even_even - even_odd, odd_even - odd_odd
            upper = members.index((group, core))
            lower = members.index((group + groups // 2, core))
            out_ref[upper, :, :HALF] = narrow(even_left + odd_left)
            out_ref[upper, :, HALF:] = narrow(even_right + odd_right)
            out_ref[lower, :, :HALF] = narrow(even_left - odd_left)
            out_ref[lower, :, HALF:] = narrow(even_right - odd_right)


def pairwise(op, values):
    while len(values) > 1:
        values = [op(*values[i : i + 2]) for i in range(0, len(values), 2)]
    return values[0]


def statistics_kernel(values_ref, level_ref, total_ref, squares_ref, largest_ref):
    scale = level_ref[...] * jnp.float32(1.0 / (NP * NP))
    count, height, width = values_ref.shape
    for row in range(0, height, 16):
        for col in range(0, width, 128):
            rows, cols = slice(row, row + 16), slice(col, col + 128)
            values = [wide(values_ref[template, rows, cols]) for template in range(count)]
            total_ref[0, rows, cols] = pairwise(jnp.add, values) * scale[:, cols]
            squares_ref[0, rows, cols] = pairwise(jnp.add, [v * v for v in values]) * (scale * scale)[:, cols]
            largest_ref[0, rows, cols] = pairwise(jnp.maximum, values) * scale[:, cols]


def call(kernel, name, outs, scratch, *operands):
    whole = pl.BlockSpec(memory_space=pltpu.VMEM)
    return pl.pallas_call(
        kernel,
        name=name,
        out_shape=outs,
        in_specs=[whole] * len(operands),
        out_specs=jax.tree.map(lambda _: whole, outs),
        scratch_shapes=scratch,
        compiler_params=pltpu.CompilerParams(vmem_limit_bytes=32 * 1024 * 1024),
    )(*operands)


def plane_place(y, core):
    return (5 * y + 4) % Y * CORES + 1 - core


def column_place(z):
    return 2 * (z % 2) + 1 - z // 2


def plane_members():
    return sorted(((y, c) for y in range(Y) for c in range(CORES)), key=lambda member: plane_place(*member))


def column_members():
    return sorted(range(Z), key=column_place)


def result_members():
    return [(z_lo * 4 + x, c) for x in (2, 3, 0, 1) for c in (1, 0) for z_lo in (1, 0)]


def receive_template(own_template, owners, spec, own_level):
    planes = [[(y * Z + z) * CORES + c for y, c in plane_members()] for z in range(Z)]
    columns = [[(y * Z + z) * CORES + c for z in column_members()] for y in range(Y) for c in range(CORES)]
    owner_z = column_place(owners // CORES % Z)
    owner_place = plane_place(owners // (Z * CORES), owners % CORES)
    owner_z, owner_place = (jnp.broadcast_to(place[:, None], (STEPS, M)) for place in (owner_z, owner_place))
    shares = own_template.reshape(PLANE, CHUNK, M)
    shares = lax.all_to_all(shares, "tile", 0, 0, axis_index_groups=planes)
    shares, spec, own_level, owner_z, owner_place = lax.optimization_barrier(
        (shares, spec, own_level, owner_z, owner_place)
    )
    spread = jax.ShapeDtypeStruct((Z, STEPS, CHUNK, M), jnp.bfloat16)
    shares = call(pick_place_kernel, "pick_place", spread, [], shares, owner_place)
    shares = lax.all_to_all(shares, "tile", 0, 0, axis_index_groups=columns)
    spread = jax.ShapeDtypeStruct((PLANE, CHUNK, M), jnp.bfloat16)
    shares = call(pick_plane_kernel, "pick_plane", spread, [], shares, owner_z)
    return lax.all_to_all(shares, "tile", 0, 0, axis_index_groups=planes), spec, own_level


def image_fields(own_tile):
    pairs = [[tile, tile + 1] for tile in range(0, lax.axis_size("tile"), CORES)]
    halves = [lax.all_gather(half, "tile", axis_index_groups=pairs) for half in (own_tile[:HALF], own_tile[HALF:])]
    return halves


def per_device(image_tiles, templates, owners):
    fwd, inv = (jnp.asarray(table) for table in make_tables())
    groups_here = lax.axis_size("orient")
    tiles = lax.axis_size("tile")
    rows_out = NP // groups_here
    spectrum = (2, NP, NP)
    fields = image_fields(image_tiles[0])
    image_outs = (jax.ShapeDtypeStruct(spectrum, jnp.bfloat16), jax.ShapeDtypeStruct((CORES, NP), jnp.float32))
    spec, levels = call(image_kernel, "image_spectrum", image_outs, [], *fields, fwd, inv)
    own_level = jnp.where(lax.axis_index("tile") % CORES == 0, levels[:1], levels[1:])
    shares, spec, own_level = receive_template(templates[0, 0], owners[0], spec, own_level)
    values = call(
        correlate_kernel,
        "correlate",
        jax.ShapeDtypeStruct((groups_here * CORES, rows_out, NP), jnp.bfloat16),
        [pltpu.VMEM((M, M), jnp.float32), pltpu.VMEM(spectrum, jnp.float32)],
        shares,
        spec,
        fwd,
        inv,
    )
    across = [[group * tiles + pair * CORES + c for group, c in result_members()] for pair in range(tiles // CORES)]
    values = lax.all_to_all(values, ("orient", "tile"), 0, 0, axis_index_groups=across)
    out = jax.ShapeDtypeStruct((1, rows_out, NP), jnp.float32)
    return call(statistics_kernel, "statistics", (out, out, out), [], values, own_level)


def solution(mesh):
    placed = (P("tile", None, None), P("orient", "tile", None, None), P("orient", None))
    return jax.shard_map(
        per_device,
        mesh=mesh,
        in_specs=placed,
        out_specs=(P("tile", "orient", None), P("tile", "orient", None), P("tile", "orient", None)),
        check_vma=False,
    )
```
